128 devices in a mesh: section: 4 (over x_hi, core), seq: 8 (over x_lo, z), mp: 4 (over y).
Axes of the slice: x: 4 (x_hi: 2, x_lo: 2; x = x_hi * 2 + x_lo), y: 4, z: 4, core: 2. Of those that a mesh axis runs over, the one named last changes fastest.
Arguments:
- features: bfloat16 [128, 257, 1280], P(('section', 'seq')), may hold values from -6 to 6
- latent_param: bfloat16 [64, 1280], replicated, may hold values from -6 to 6
- query_proj: bfloat16 [1280, 1536], P(None, 'mp'), may hold values from -0.15625 to 0.15625
- key_proj: bfloat16 [1280, 1536], P(None, 'mp'), may hold values from -0.15625 to 0.15625
- value_proj: bfloat16 [1280, 1536], P(None, 'mp'), may hold values from -0.15625 to 0.15625
- out_proj: bfloat16 [1536, 1280], P('mp'), may hold values from -0.15625 to 0.15625
- hidden: bfloat16 [4, 1024, 8192], P(None, 'seq', 'mp'), may hold values from -6 to 6
- key_weight: bfloat16 [4, 1280, 8192], P('section', None, 'mp'), may hold values from -0.15625 to 0.15625
- value_weight: bfloat16 [4, 1280, 8192], P('section', None, 'mp'), may hold values from -0.15625 to 0.15625
- gate_angle: float32 [4], P('section'), may hold values from 0.3 to 1.5
- group_images: int32 [4, 8, 4], P(None, 'seq'), may hold values from 0 to 31, as said below
- token_slot: int32 [4, 8, 128], P(None, 'seq'), may hold values from 0 to 3, never falling along the last dimension, each value on 1 to 64 neighbouring positions
- attend: int32 [4, 8, 128], P(None, 'seq'), may hold values 0 or 1
Outputs:
- states: bfloat16 [4, 4, 1024, 8192], P('section', None, 'seq', 'mp')
The draws below stay inside these ranges and needn't reach their ends.
Inputs may be any that keep to these rules, and one draw needn't show every extreme that they name: `group_images`: the 4 entries of a group are consecutive image numbers of its micro-batch, not falling from group to group; the first group of every micro-batch starts at image 0, and in micro-batch 0 the last group ends at image 32 - 1. The entries of group c lie between 4 * (c - 1) and 4 * (c + 2) - 1.
All inputs are finite; a program needn't handle non-finite values. No bound on the sum of `attend` on one device may be relied on, other than what follows from the above.
Results may differ from the reference program's by a relative error of at most 0.007.
Values may be sent and summed in bfloat16 or wider, within the bound.
No kernel may reach another device: no remote copies, remote signals or barrier semaphores. Data moves between devices by JAX's collectives and lax.ppermute only.
A program may use at most 192 MiB of HBM per device.

```python
import math
import jax
import jax.numpy as jnp
import numpy as np
from jax import lax

D = 8192
HEAD = 128
VDIM = 1280
LATENTS = 64
PHEADS = 16
PHEAD = 96
PATCHES = 257
GROUP = 128
W = 4
MB = 4
IMAGES = 128
IMG_SEQ = 32
SEQLEN = 1024
N_SECTION = 4
N_SEQ = 8


def draw_group_images(key, part):
    key = jax.random.fold_in(key, 5)
    step = IMG_SEQ // N_SEQ
    group_pos = jnp.arange(N_SEQ, dtype=jnp.int32)
    batch_pos = jnp.arange(MB, dtype=jnp.int32)
    starts = group_pos * step - 1
    jitter = jax.random.randint(key, (MB, N_SEQ), -1, 2, dtype=jnp.int32)
    first = jnp.clip(starts[None, :] + jitter, 0, IMG_SEQ - W)
    first = jnp.where(group_pos[None, :] == 0, 0, first)
    pinned = (batch_pos[:, None] == 0) & (group_pos[None, :] == N_SEQ - 1)
    first = jnp.where(pinned, IMG_SEQ - W, first)
    first = jax.lax.cummax(first, axis=1)
    return (first[:, :, None] + jnp.arange(W, dtype=jnp.int32)[None, None, :]).astype(jnp.int32)


def set_ends(entries, rng, least, high):
    shape = entries.shape
    index_at = [jax.random.randint(jax.random.fold_in(rng, axis), (), 0, shape[axis]) for axis in range(len(shape))]
    entries = entries.at[tuple(index_at)].set(least)
    longest = shape.index(max(shape))
    index_at[longest] = (index_at[longest] + 1) % shape[longest]
    return entries.at[tuple(index_at)].set(high)


def block_scale(stream_key, shape, shards, least, top_value):
    level, own = 1.0, jax.random.fold_in(stream_key, 6)
    for position, shards_of in shards:
        draws = jnp.exp(jax.random.uniform(jax.random.fold_in(own, position), (shards_of,), jnp.float32, least / len(shards), top_value / len(shards)))
        level = level * jnp.repeat(draws, shape[position] // shards_of).reshape([-1 if axis == position else 1 for axis in range(len(shape))])
    return level


def profile(amount, total, bound, skew):
    weights = [(1 << 20) // math.isqrt(rank ** skew) + 1 for rank in range(2, amount + 1)]
    spare, holding = total - bound - (amount - 1), [1] * (amount - 1)
    while spare > 0:
        movable = [i for i in range(amount - 1) if holding[i] < bound]
        whole, remaining = sum([weights[i] for i in movable]), spare
        for i in movable:
            extra = min(bound - holding[i], max(1, remaining * weights[i] // whole), spare)
            holding[i] = holding[i] + extra
            spare = spare - extra
    return np.array([bound] + holding)


def ragged(rng, amount, total, most, slope):
    if amount == 2:
        one = jax.random.randint(rng, (), max(1, total - most), min(most, total - 1) + 1)
        return jnp.stack([one, total - one])
    tallies = jnp.asarray(profile(amount, total, most, slope), jnp.int32)
    couples = (amount - 1) // 2
    donor, sink = tallies[1:1 + 2 * couples:2], tallies[2:2 + 2 * couples:2]
    room = jnp.minimum(donor - 1, most - sink)
    passed = jax.random.randint(jax.random.fold_in(rng, 1), (couples,), 0, 1 << 20) % (room + 1)
    tallies = tallies.at[1:1 + 2 * couples:2].set(donor - passed).at[2:2 + 2 * couples:2].set(sink + passed)
    return tallies[jax.random.permutation(jax.random.fold_in(rng, 2), amount)]


def centred(rng, extent, scale, reach, pieces=(), kind=jnp.bfloat16):
    level = block_scale(rng, extent, pieces, -0.22, 0.18) if pieces else 1.0
    entries = jax.random.normal(rng, extent, jnp.float32) * scale * level
    return jnp.minimum(jnp.maximum(entries, -reach), reach).astype(kind)


def setup_inputs(seed: int = 0) -> dict:
    key_of = jax.random.split(jax.random.key(seed), 14)
    features = centred(key_of[0], (IMAGES, PATCHES, VDIM), 1.0, 6.0, ((0, 32),))
    latent_param = centred(key_of[1], (LATENTS, VDIM), 1.0, 6.0)
    query_proj = centred(key_of[2], (VDIM, PHEADS * PHEAD), VDIM ** -0.5, 0.15625, ((1, 4),))
    key_proj = centred(key_of[3], (VDIM, PHEADS * PHEAD), VDIM ** -0.5, 0.15625, ((1, 4),))
    value_proj = centred(key_of[4], (VDIM, PHEADS * PHEAD), VDIM ** -0.5, 0.15625, ((1, 4),))
    out_proj = centred(key_of[5], (PHEADS * PHEAD, VDIM), (PHEADS * PHEAD) ** -0.5, 0.15625, ((0, 4),))
    hidden = centred(key_of[6], (MB, SEQLEN, D), 1.0, 6.0, ((1, 8), (2, 4)))
    key_weight = centred(key_of[7], (N_SECTION, VDIM, D), VDIM ** -0.5, 0.15625, ((0, 4), (2, 4)))
    value_weight = centred(key_of[8], (N_SECTION, VDIM, D), VDIM ** -0.5, 0.15625, ((0, 4), (2, 4)))
    gate_angle = jnp.clip(0.3 + 1.2 * jax.random.uniform(key_of[9], (N_SECTION,), jnp.float32) ** block_scale(key_of[9], (N_SECTION,), ((0, 4),), -0.2, 0.2), 0.3, 1.5)
    group_images = draw_group_images(jax.random.fold_in(key_of[13], 71), 0)
    token_slot = jax.vmap(lambda own: jnp.searchsorted(jnp.cumsum(ragged(own, W, GROUP, GROUP // 2, 1)), jnp.arange(GROUP), side="right"))(jax.random.split(key_of[11], MB * N_SEQ)).reshape((MB, N_SEQ, GROUP)).astype(jnp.int32)
    attend = set_ends((jax.random.randint(key_of[12], (MB, N_SEQ, GROUP), 0, 8) < 7).astype(jnp.int32), jax.random.fold_in(key_of[12], 1), 0, 1)
    return dict(features=features, latent_param=latent_param, query_proj=query_proj, key_proj=key_proj, value_proj=value_proj, out_proj=out_proj, hidden=hidden, key_weight=key_weight, value_weight=value_weight, gate_angle=gate_angle, group_images=group_images, token_slot=token_slot, attend=attend)


def normalize(v):
    mean = lax.optimization_barrier(jnp.mean(v, axis=-1, keepdims=True))
    cent = v - mean
    var = lax.optimization_barrier(jnp.mean(cent * cent, axis=-1, keepdims=True))
    return cent * lax.rsqrt(var + 1e-05)

def reference(features, latent_param, query_proj, key_proj, value_proj, out_proj, hidden, key_weight, value_weight, gate_angle, group_images, token_slot, attend):
    lat_start = latent_param.astype(jnp.float32)
    base = normalize(lat_start).astype(jnp.bfloat16)
    pquery = jnp.dot(base, query_proj, preferred_element_type=jnp.float32).astype(jnp.bfloat16)
    pquery = pquery.astype(jnp.float32).reshape(LATENTS, PHEADS, PHEAD)

    def resample(feat):
        context = normalize(feat.astype(jnp.float32)).astype(jnp.bfloat16)
        stacked = jnp.concatenate([context, base], axis=0)
        pkey = jnp.dot(stacked, key_proj, preferred_element_type=jnp.float32).astype(jnp.bfloat16)
        pval = jnp.dot(stacked, value_proj, preferred_element_type=jnp.float32).astype(jnp.bfloat16)
        pkey = pkey.astype(jnp.float32).reshape(-1, PHEADS, PHEAD)
        pval = pval.astype(jnp.float32).reshape(-1, PHEADS, PHEAD)
        score = jnp.einsum('lhd,khd->hlk', pquery, pkey) * PHEAD ** (-0.5)
        weight = jax.nn.softmax(score, axis=-1).astype(jnp.bfloat16).astype(jnp.float32)
        mixed = jnp.einsum('hlk,khd->lhd', weight, pval).reshape(LATENTS, PHEADS * PHEAD).astype(jnp.bfloat16)
        update = jnp.dot(mixed, out_proj, preferred_element_type=jnp.float32)
        return normalize(lat_start + update).astype(jnp.bfloat16)
    every = lax.map(resample, features)
    key_slot = jnp.arange(W * LATENTS, dtype=jnp.int32) // LATENTS
    heads = D // HEAD
    results = []
    current = hidden
    for section in range(N_SECTION):
        gate = jnp.tanh(gate_angle[section])
        outs = []
        for batch in range(MB):

            def one(args):
                block, ids, slot, alive = args
                chosen = every[batch * IMG_SEQ + ids].reshape(W * LATENTS, VDIM)
                keys = jnp.dot(chosen, key_weight[section], preferred_element_type=jnp.float32).astype(jnp.bfloat16)
                vals = jnp.dot(chosen, value_weight[section], preferred_element_type=jnp.float32).astype(jnp.bfloat16)
                xf = block.astype(jnp.float32)
                msq = lax.optimization_barrier(jnp.mean(xf * xf, axis=-1, keepdims=True))
                xn = (xf * lax.rsqrt(msq + 1e-05)).astype(jnp.bfloat16)
                qh = xn.astype(jnp.float32).reshape(GROUP, heads, HEAD)
                kh = keys.astype(jnp.float32).reshape(W * LATENTS, heads, HEAD)
                vh = vals.astype(jnp.float32).reshape(W * LATENTS, heads, HEAD)
                score = jnp.einsum('thd,khd->htk', qh, kh) * HEAD ** (-0.5)
                allowed = key_slot[None, :] == slot[:, None]
                score = jnp.where(allowed[None], score, -1e+30)
                weight = jax.nn.softmax(score, axis=-1).astype(jnp.bfloat16).astype(jnp.float32)
                attn = jnp.einsum('htk,khd->thd', weight, vh).reshape(GROUP, D)
                live = alive.astype(jnp.float32)[:, None]
                return (xf + gate * live * attn).astype(jnp.bfloat16)
            blocks = current[batch].reshape(N_SEQ, GROUP, D)
            out = lax.map(one, (blocks, group_images[batch], token_slot[batch], attend[batch]))
            outs.append(out.reshape(SEQLEN, D))
        current = jnp.stack(outs)
        results.append(current)
    return jnp.stack(results)
```

```python
import functools

import jax
import jax.numpy as jnp
from jax import lax
from jax.experimental import pallas as pl
from jax.experimental.pallas import tpu as pltpu
from jax.sharding import PartitionSpec as P

D = 8192
HEAD = 128
LATENTS = 64
PHEAD = 96
EPS = 1e-05
NEG = -1e30
F32 = jnp.float32
BF16 = jnp.bfloat16
VMEM_LIMIT = 40 * 1024 * 1024


def normalize(v):
    mean = jnp.mean(v, axis=-1, keepdims=True)
    cent = v - mean
    var = jnp.mean(cent * cent, axis=-1, keepdims=True)
    return cent * lax.rsqrt(var + EPS)


def dot(a, b):
    return jnp.dot(a, b, preferred_element_type=F32)


def dot_nt(a, b):
    return lax.dot_general(a, b, (((1,), (1,)), ((), ())), preferred_element_type=F32)


def up16(n):
    return -(-n // 16) * 16


def up128(n):
    return -(-n // 128) * 128


def resample_kernel(n, ids, feat, lat, qp, kp, vp, op, *rest):
    outs = rest[:n]
    ctx, pk, pv, pqm = rest[n:]
    patches = feat.shape[1]
    inner = qp.shape[1]
    heads = inner // PHEAD
    rows = ctx.shape[0]
    keys = LATENTS + patches
    step = pl.program_id(0)

    def head_of(shape):
        return lax.broadcasted_iota(jnp.int32, shape, 1) // PHEAD

    @pl.when(step == 0)
    def _():
        base = normalize(lat[...].astype(F32)).astype(BF16)
        pq = dot(base, qp[...]).astype(BF16).astype(F32)
        which = head_of((LATENTS, inner))
        for h in range(heads):
            pqm[h * LATENTS : (h + 1) * LATENTS, :] = jnp.where(which == h, pq, 0.0).astype(BF16)
        pk[0:LATENTS, :] = dot(base, kp[...]).astype(BF16)
        pv[0:LATENTS, :] = dot(base, vp[...]).astype(BF16)
        pad = pk.shape[0] - LATENTS - rows
        if pad:
            pk[LATENTS + rows :, :] = jnp.zeros((pad, inner), BF16)
            pv[LATENTS + rows :, :] = jnp.zeros((pad, inner), BF16)
        ctx[rows - 16 :, :] = jnp.zeros((16, ctx.shape[1]), BF16)

    for r in range(0, patches, 64):
        end = min(r + 64, patches)
        ctx[r:end, :] = normalize(feat[0, r:end, :].astype(F32)).astype(BF16)
    pk[LATENTS : LATENTS + rows, :] = dot(ctx[...], kp[...]).astype(BF16)
    pv[LATENTS : LATENTS + rows, :] = dot(ctx[...], vp[...]).astype(BF16)

    score = dot_nt(pqm[...], pk[...]) * PHEAD ** (-0.5)
    lane = lax.broadcasted_iota(jnp.int32, score.shape, 1)
    score = jnp.where(lane < keys, score, NEG)
    e = jnp.exp(score - jnp.max(score, axis=1, keepdims=True))
    weight = (e / jnp.sum(e, axis=1, keepdims=True)).astype(BF16)
    mix = dot(weight, pv[...])
    which = head_of((LATENTS, inner))
    mixed = jnp.zeros((LATENTS, inner), F32)
    for h in range(heads):
        mixed = jnp.where(which == h, mix[h * LATENTS : (h + 1) * LATENTS, :], mixed)
    update = dot(mixed.astype(BF16), op[...])
    for i in range(n):

        @pl.when(step == i)
        def _(i=i):
            outs[i][...] = update.astype(outs[i].dtype)


def resample(ids, features, latent_param, qp, kp, vp, op, dtype):
    n = ids.shape[0]
    _, patches, vdim = features.shape
    inner = qp.shape[1]
    heads = inner // PHEAD
    rows = up16(patches)
    padded = up128(LATENTS + rows)
    whole = lambda a: pl.BlockSpec(a.shape, lambda i, s: (0,) * a.ndim)
    out = jax.ShapeDtypeStruct((LATENTS, vdim), dtype)
    return pl.pallas_call(
        functools.partial(resample_kernel, n),
        out_shape=[out] * n,
        grid_spec=pltpu.PrefetchScalarGridSpec(
            num_scalar_prefetch=1,
            grid=(n,),
            in_specs=[
                pl.BlockSpec((1, patches, vdim), lambda i, s: (s[i], 0, 0)),
                whole(latent_param),
                whole(qp),
                whole(kp),
                whole(vp),
                whole(op),
            ],
            out_specs=[pl.BlockSpec((LATENTS, vdim), lambda i, s: (0, 0))] * n,
            scratch_shapes=[
                pltpu.VMEM((rows, vdim), BF16),
                pltpu.VMEM((padded, inner), BF16),
                pltpu.VMEM((padded, inner), BF16),
                pltpu.VMEM((heads * LATENTS, inner), BF16),
            ],
        ),
        compiler_params=pltpu.CompilerParams(vmem_limit_bytes=VMEM_LIMIT),
        cost_estimate=pl.CostEstimate(
            flops=n * 2 * (rows * vdim * 2 * inner + 3 * heads * LATENTS * padded * inner),
            bytes_accessed=n * patches * vdim * 2 + 4 * vdim * inner * 2,
            transcendentals=n * heads * LATENTS * padded,
        ),
        name="resample",
    )(ids, features, latent_param, qp, kp, vp, op)


def combine_kernel(lat, own, a, b, c, out):
    total = own[...] + a[...].astype(F32) + b[...].astype(F32) + c[...].astype(F32)
    out[...] = normalize(lat[...].astype(F32) + total).astype(BF16)


def combine(latent_param, own, parts):
    return pl.pallas_call(
        combine_kernel,
        out_shape=jax.ShapeDtypeStruct(latent_param.shape, BF16),
        name="combine",
    )(latent_param, own, *parts)


def project_kernel(flags, a0, a1, a2, a3, kw0, vw0, kw1, vw1, keys, vals, chosen):
    @pl.when(pl.program_id(0) == 0)
    def _():
        for i, a in enumerate((a0, a1, a2, a3)):
            chosen[i * LATENTS : (i + 1) * LATENTS, :] = a[...]

    @pl.when(flags[0] == 0)
    def _():
        keys[...] = dot(chosen[...], kw0[0]).astype(BF16)
        vals[...] = dot(chosen[...], vw0[0]).astype(BF16)

    @pl.when(flags[0] != 0)
    def _():
        keys[...] = dot(chosen[...], kw1[0]).astype(BF16)
        vals[...] = dot(chosen[...], vw1[0]).astype(BF16)


def project(flag, chunks, own, other, tile=256):
    vdim, width = own[0].shape[1:]
    rows = len(chunks) * LATENTS
    chunk = pl.BlockSpec((LATENTS, vdim), lambda i, s: (0, 0))
    w0 = pl.BlockSpec((1, vdim, tile), lambda i, s: (0, 0, i * (1 - s[0])))
    w1 = pl.BlockSpec((1, vdim, tile), lambda i, s: (0, 0, i * s[0]))
    out = pl.BlockSpec((rows, tile), lambda i, s: (0, i))
    shape = jax.ShapeDtypeStruct((rows, width), BF16)
    return pl.pallas_call(
        project_kernel,
        out_shape=[shape, shape],
        grid_spec=pltpu.PrefetchScalarGridSpec(
            num_scalar_prefetch=1,
            grid=(width // tile,),
            in_specs=[chunk] * 4 + [w0, w0, w1, w1],
            out_specs=[out, out],
            scratch_shapes=[pltpu.VMEM((rows, vdim), BF16)],
        ),
        compiler_params=pltpu.CompilerParams(vmem_limit_bytes=VMEM_LIMIT),
        cost_estimate=pl.CostEstimate(
            flops=4 * rows * vdim * width,
            bytes_accessed=4 * vdim * width + 4 * rows * width,
            transcendentals=0,
        ),
        name="project",
    )(flag, *chunks, own[0], own[1], other[0], other[1])


def layer_kernel(parts, row, ids, x, keys, vals, meta, *rest):
    squares = rest[:parts]
    y, square_out, scale_s, bias_s, high_s, gate_s, acc = rest[parts:]
    step = pl.program_id(0)
    rows = x.shape[1]
    heads = x.shape[2] // HEAD

    @pl.when(step == 0)
    def _():
        total = squares[0][...]
        for part in squares[1:]:
            total = total + part[...]
        scale = lax.rsqrt(total / D + EPS) * HEAD ** (-0.5)
        tile = jnp.concatenate(
            [scale, meta[0:1, :], meta[row : row + 1, :], jnp.zeros((rows - 3, rows), F32)], axis=0
        )
        cols = tile.T
        slot = jnp.broadcast_to(cols[:, 1:2], (rows, HEAD))
        scale_s[...] = jnp.broadcast_to(cols[:, 0:1], (rows, HEAD))
        gate_s[...] = jnp.broadcast_to(cols[:, 2:3], (rows, HEAD))
        high = jnp.where(slot > 1.5, 1.0, 0.0)
        high_s[...] = high
        half = (lax.broadcasted_iota(jnp.int32, (rows, HEAD), 1) // LATENTS).astype(F32)
        bias_s[...] = jnp.where(slot - 2.0 * high == half, 0.0, NEG)
        acc[...] = jnp.zeros_like(acc)

    high = high_s[...] > 0.5
    for h in range(heads):
        cols = slice(h * HEAD, (h + 1) * HEAD)
        q = x[0, :, cols]
        score = dot_nt(q, keys[:, cols])
        t = jnp.where(high, score[:, HEAD:], score[:, :HEAD]) * scale_s[...] + bias_s[...]
        e = jnp.exp(t - jnp.max(t, axis=1, keepdims=True))
        w = e / jnp.sum(e, axis=1, keepdims=True)
        weight = jnp.concatenate([jnp.where(high, 0.0, w), jnp.where(high, w, 0.0)], axis=1)
        attn = dot(weight.astype(BF16), vals[:, cols])
        out = (q.astype(F32) + gate_s[...] * attn).astype(BF16)
        y[:, cols] = out
        of = out.astype(F32)
        acc[...] += of * of

    @pl.when(step == pl.num_programs(0) - 1)
    def _():
        square_out[...] = jnp.sum(acc[...].T, axis=0, keepdims=True)


def layer(row, index, x, kv, meta, squares, tile=512):
    keys, vals = kv
    _, rows, width = x.shape
    nkeys = keys.shape[0]
    block = pl.BlockSpec((nkeys, tile), lambda i, s: (0, i))
    whole = lambda a: pl.BlockSpec(a.shape, lambda i, s: (0, 0))
    scratch = pltpu.VMEM((rows, HEAD), F32)
    return pl.pallas_call(
        functools.partial(layer_kernel, len(squares), row),
        out_shape=[
            jax.ShapeDtypeStruct((rows, width), BF16),
            jax.ShapeDtypeStruct((1, rows), F32),
        ],
        grid_spec=pltpu.PrefetchScalarGridSpec(
            num_scalar_prefetch=1,
            grid=(width // tile,),
            in_specs=[
                pl.BlockSpec((1, rows, tile), lambda i, s: (s[0], 0, i)),
                block,
                block,
                whole(meta),
            ]
            + [whole(a) for a in squares],
            out_specs=[
                pl.BlockSpec((rows, tile), lambda i, s: (0, i)),
                pl.BlockSpec((1, rows), lambda i, s: (0, 0)),
            ],
            scratch_shapes=[scratch] * 5,
        ),
        compiler_params=pltpu.CompilerParams(vmem_limit_bytes=VMEM_LIMIT),
        cost_estimate=pl.CostEstimate(
            flops=4 * rows * nkeys * width * 4,
            bytes_accessed=2 * (2 * nkeys * width + 2 * rows * width),
            transcendentals=rows * width,
        ),
        name="layer",
    )(index, x, keys, vals, meta, *squares)


def body(
    features,
    latent_param,
    query_proj,
    key_proj,
    value_proj,
    out_proj,
    hidden,
    key_weight,
    value_weight,
    gate_angle,
    group_images,
    token_slot,
    attend,
):
    s = lax.axis_index("section")
    c = lax.axis_index("seq")
    m = lax.axis_index("mp")
    core = s & 1
    far = s >> 1
    mates = lax.axis_size("mp")
    seqs = lax.axis_size("seq")
    sections = lax.axis_size("section")

    def mp_shift(a, k):
        return lax.ppermute(a, "mp", [(i, (i + k) % mates) for i in range(mates)])

    def core_swap(a):
        return lax.ppermute(a, "section", [(i, i ^ 1) for i in range(sections)])

    def far_swap(a):
        return lax.ppermute(a, "section", [(i, i ^ 2) for i in range(sections)])

    def cross(a):
        return lax.ppermute(a, "section", [(0, 2), (1, 3)])

    def spread(a):
        return [a] + [mp_shift(a, k) for k in (1, 2, 3)]

    own_w = (key_weight, value_weight)
    other_w = (core_swap(key_weight), core_swap(value_weight))
    gate_own = jnp.broadcast_to(jnp.tanh(gate_angle)[:, None], (1, 128))
    gate_other = core_swap(gate_own)
    gate_first = jnp.where(core == 0, gate_own, gate_other)
    gate_second = jnp.where(core == 0, gate_other, gate_own)

    order = jnp.stack([(m + 2) & 3, (m + 1) & 3, (m + 3) & 3]).astype(jnp.int32)
    weights = (query_proj, key_proj, value_proj, out_proj)
    p2, p1, p3 = resample(order, features, latent_param, *weights, BF16)
    r2, r1, r3 = mp_shift(p2, 2), mp_shift(p1, 1), mp_shift(p3, 3)
    (p0,) = resample(m[None].astype(jnp.int32), features, latent_param, *weights, F32)
    latents = combine(latent_param, p0, (r1, r2, r3))

    hf = hidden.astype(F32)
    entering = jnp.sum(hf * hf, axis=-1)
    entering = sum(spread(entering))

    left = lax.ppermute(latents, "seq", [(i, i + 1) for i in range(seqs - 1)])
    right = lax.ppermute(latents, "seq", [(i + 1, i) for i in range(seqs - 1)])
    firsts = group_images[:, 0, 0]
    start = lax.dynamic_index_in_dim(firsts, s, 0, keepdims=False)
    where_is = ((start + ((m - start) & 3)) >> 2) - c
    picked = jnp.where(where_is == 0, latents, jnp.where(where_is < 0, left, right))
    chosen_own = spread(picked)
    chosen_far = spread(far_swap(picked))

    block = (m - firsts[:, None] - token_slot[:, 0, :]) & 3
    alive = attend[:, 0, :].astype(F32)
    rows = jnp.stack(
        [block.astype(F32), alive * gate_first, alive * gate_second]
        + [jnp.zeros_like(alive)] * 5,
        axis=1,
    )
    meta_own = lax.dynamic_index_in_dim(rows, s, 0, keepdims=False)
    meta_far = lax.dynamic_index_in_dim(rows, s ^ 2, 0, keepdims=False)

    flag_first = core[None].astype(jnp.int32)
    flag_second = (1 - core)[None].astype(jnp.int32)
    first_own = project(flag_first, chosen_own, own_w, other_w)
    first_far = project(flag_first, chosen_far, own_w, other_w)
    second_own = project(flag_second, chosen_own, own_w, other_w)
    second_far = project(flag_second, chosen_far, own_w, other_w)

    zero = jnp.zeros((1,), jnp.int32)
    batch0 = core[None].astype(jnp.int32)
    batch1 = batch0 + 2

    sq0 = lax.dynamic_slice_in_dim(entering, core, 1, 0)
    sq1 = lax.dynamic_slice_in_dim(entering, core + 2, 1, 0)
    a0, qa0 = layer(1, batch0, hidden, first_own, meta_own, [sq0])
    qa0 = spread(qa0)
    a1, qa1 = layer(1, batch1, hidden, first_far, meta_far, [sq1])
    qa1 = spread(qa1)
    b0, qb0 = layer(2, zero, a0[None], second_own, meta_own, qa0)
    x0 = cross(b0)
    qb0 = cross(sum(spread(qb0)))
    b1, qb1 = layer(2, zero, a1[None], second_far, meta_far, qa1)
    x1 = cross(b1)
    qb1 = cross(sum(spread(qb1)))

    c0, qc0 = layer(1, zero, x0[None], first_far, meta_far, [qb0])
    qc0 = spread(qc0)
    c1, qc1 = layer(1, zero, x1[None], first_own, meta_own, [qb1])
    qc1 = spread(qc1)
    d0, _ = layer(2, zero, c0[None], second_far, meta_far, qc0)
    d1, _ = layer(2, zero, c1[None], second_own, meta_own, qc1)

    def split(a, b, c_, d_):
        first = jnp.where(far == 0, a, c_)
        second = jnp.where(far == 0, b, d_)
        keep = jnp.where(core == 0, first, second)
        send = jnp.where(core == 0, second, first)
        return keep, core_swap(send)

    keep0, got0 = split(a0, b0, c0, d0)
    keep1, got1 = split(a1, b1, c1, d1)
    even = core == 0
    return jnp.stack(
        [
            jnp.where(even, keep0, got0),
            jnp.where(even, got0, keep0),
            jnp.where(even, keep1, got1),
            jnp.where(even, got1, keep1),
        ]
    )[None]


def solution(mesh):
    return jax.shard_map(
        body,
        mesh=mesh,
        in_specs=(
            P(("section", "seq"), None, None),
            P(),
            P(None, "mp"),
            P(None, "mp"),
            P(None, "mp"),
            P("mp", None),
            P(None, "seq", "mp"),
            P("section", None, "mp"),
            P("section", None, "mp"),
            P("section"),
            P(None, "seq", None),
            P(None, "seq", None),
            P(None, "seq", None),
        ),
        out_specs=P("section", None, "seq", "mp"),
        check_vma=False,
    )
```

```python
import functools

import jax
import jax.numpy as jnp
from jax import lax
from jax.experimental import pallas as pl
from jax.experimental.pallas import tpu as pltpu
from jax.sharding import PartitionSpec as P

D = 8192
HEAD = 128
LATENTS = 64
PHEAD = 96
EPS = 1e-05
NEG = -1e30
LOG2E = 1.4426950408889634
F32 = jnp.float32
BF16 = jnp.bfloat16
MIB = 1024 * 1024
SPARE = 16


def normalize(v):
    mean = jnp.mean(v, axis=-1, keepdims=True)
    cent = v - mean
    var = jnp.mean(cent * cent, axis=-1, keepdims=True)
    return cent * lax.rsqrt(var + EPS)


def dot(a, b):
    return jnp.dot(a, b, preferred_element_type=F32)


def dot_nt(a, b):
    return lax.dot_general(a, b, (((1,), (1,)), ((), ())), preferred_element_type=F32)


def up16(n):
    return -(-n // 16) * 16


def up128(n):
    return -(-n // 128) * 128


def near(a):
    return pltpu.with_memory_space_constraint(a, pltpu.VMEM)


def away(a):
    return pltpu.with_memory_space_constraint(a, pltpu.HBM)


IN_VMEM = pl.BlockSpec(memory_space=pltpu.VMEM)
IN_SMEM = pl.BlockSpec(memory_space=pltpu.SMEM)
IN_HBM = pl.BlockSpec(memory_space=pltpu.HBM)


def prepare(lat, qp, kp, vp, tail, ctx, pk, pv, pqm):
    inner = qp.shape[1]
    heads = inner // PHEAD
    rows = ctx.shape[0]
    cut = inner // 256 * 256
    side = inner - cut
    tail[:, :side] = kp[:, cut:]
    tail[:, side:] = vp[:, cut:]
    base = normalize(lat[...].astype(F32)).astype(BF16)
    pq = dot(base, qp[...]).astype(BF16).astype(F32)
    which = lax.broadcasted_iota(jnp.int32, (LATENTS, inner), 1) // PHEAD
    for h in range(heads):
        pqm[h * LATENTS : (h + 1) * LATENTS, :] = jnp.where(which == h, pq, 0.0).astype(BF16)
    project_rows(base, 0, kp, vp, tail, pk, pv)
    pad = pk.shape[0] - LATENTS - rows
    if pad:
        pk[LATENTS + rows :, :] = jnp.zeros((pad, inner), BF16)
        pv[LATENTS + rows :, :inner] = jnp.zeros((pad, inner), BF16)
    pv[:, inner:] = jnp.ones((pv.shape[0], 128), BF16)
    ctx[rows - 16 :, :] = jnp.zeros((16, ctx.shape[1]), BF16)


def project_rows(a, at, kp, vp, tail, pk, pv):
    stop = at + a.shape[0]
    inner = kp.shape[1]
    cut = inner // 256 * 256
    side = inner - cut
    pk[at:stop, :cut] = dot(a, kp[:, :cut]).astype(BF16)
    pv[at:stop, :cut] = dot(a, vp[:, :cut]).astype(BF16)
    both = dot(a, tail[...]).astype(BF16)
    pk[at:stop, cut:] = both[:, :side]
    pv[at:stop, cut:inner] = both[:, side:]


def one_image(frame, kp, vp, op, tail, ctx, pk, pv, pqm):
    patches = frame.shape[0]
    inner = kp.shape[1]
    keys = LATENTS + patches
    for r in range(0, patches, 64):
        end = min(r + 64, patches)
        ctx[r:end, :] = normalize(frame[r:end, :].astype(F32)).astype(BF16)
    project_rows(ctx[...], LATENTS, kp, vp, tail, pk, pv)
    score = dot_nt(pqm[...], pk[...]) * (PHEAD ** (-0.5) * LOG2E)
    lane = lax.broadcasted_iota(jnp.int32, score.shape, 1)
    score = jnp.where(lane < keys, score, NEG)
    e = jnp.exp2(score - jnp.max(score, axis=1, keepdims=True)).astype(BF16)
    mix = dot(e, pv[...])
    inverse = 1.0 / mix[:, inner:]
    tiles = []
    for j in range(inner // 128):
        at = lax.broadcasted_iota(jnp.int32, (LATENTS, 128), 1) + j * 128
        tile = jnp.zeros((LATENTS, 128), F32)
        for h in range(j * 128 // PHEAD, (j * 128 + 127) // PHEAD + 1):
            rows_h = slice(h * LATENTS, (h + 1) * LATENTS)
            value = mix[rows_h, j * 128 : (j + 1) * 128] * inverse[rows_h, :]
            tile = jnp.where(at // PHEAD == h, value, tile)
        tiles.append(tile.astype(BF16))
    return dot(jnp.concatenate(tiles, axis=1), op[...])


def resample_scratch(patches, vdim, inner):
    rows = up16(patches)
    padded = up128(LATENTS + rows)
    cut = inner // 256 * 256
    return [
        pltpu.VMEM((vdim, 2 * (inner - cut)), BF16),
        pltpu.VMEM((rows, vdim), BF16),
        pltpu.VMEM((padded, inner), BF16),
        pltpu.VMEM((padded, inner + 128), BF16),
        pltpu.VMEM((inner // PHEAD * LATENTS, inner), BF16),
    ]


def resample_sent_kernel(n, ids, lat, feat, hid, *rest):
    weights, rest = rest[:4], rest[4:]
    sent, squares, rest = rest[:n], rest[n], rest[n + 1 :]
    held, (frames, updates, hid0, hid1), work, sems = rest[:4], rest[4:8], rest[8:-1], rest[-1]
    qp, kp, vp, op = held
    loads = [pltpu.make_async_copy(a, b, sems.at[i]) for i, (a, b) in enumerate(zip(weights, held))]
    loads.append(pltpu.make_async_copy(hid.at[ids[n]], hid0, sems.at[4]))
    loads.append(pltpu.make_async_copy(hid.at[ids[n] + 2], hid1, sems.at[5]))
    images = [pltpu.make_async_copy(feat.at[ids[i]], frames.at[i], sems.at[6 + i]) for i in range(n)]
    for load in loads[:3] + images + loads[3:]:
        load.start()
    for load in loads[:3]:
        load.wait()
    prepare(lat, qp, kp, vp, *work)
    for load in images + loads[3:4]:
        load.wait()

    def step(i, carry):
        updates[i] = one_image(frames.at[i], kp, vp, op, *work).astype(BF16)
        return carry

    lax.fori_loop(0, n, step, 0)
    lines = []
    for load, a in zip(loads[4:], (hid0, hid1)):
        load.wait()
        acc = jnp.zeros((a.shape[0], 128), F32)
        for at in range(0, a.shape[1], 128):
            v = a[:, at : at + 128].astype(F32)
            acc = acc + v * v
        lines.append(jnp.sum(acc.T, axis=0, keepdims=True))
    squares[...] = jnp.concatenate(lines, axis=0)
    high = [line.astype(BF16).astype(F32) for line in lines]
    low = [line - h for line, h in zip(lines, high)]
    spare = jnp.zeros((1, sent[0].shape[1] - 4 * 128), F32)
    line = jnp.concatenate(high + low + [spare], axis=1)
    first = lax.broadcasted_iota(jnp.int32, (SPARE, line.shape[1]), 0) == 0
    line = jnp.where(first, line, 0.0).astype(BF16)
    for i in range(n):
        sent[i][0:LATENTS, :] = updates[i]
        sent[i][LATENTS:, :] = line


def resample_sent(ids, features, latent_param, hidden, weights):
    n = ids.shape[0] - 1
    _, patches, vdim = features.shape
    _, rows, width = hidden.shape
    inner = weights[0].shape[1]
    return pl.pallas_call(
        functools.partial(resample_sent_kernel, n),
        out_shape=[pltpu.VMEM((LATENTS + SPARE, vdim), BF16)] * n
        + [pltpu.VMEM((2, rows), F32)],
        in_specs=[IN_SMEM, IN_VMEM] + [IN_HBM] * 6,
        out_specs=[IN_VMEM] * (n + 1),
        scratch_shapes=[pltpu.VMEM(w.shape, BF16) for w in weights]
        + [
            pltpu.VMEM((n, patches, vdim), BF16),
            pltpu.VMEM((n, LATENTS, vdim), BF16),
            pltpu.VMEM((rows, width), BF16),
            pltpu.VMEM((rows, width), BF16),
        ]
        + resample_scratch(patches, vdim, inner)
        + [pltpu.SemaphoreType.DMA((6 + n,))],
        compiler_params=pltpu.CompilerParams(vmem_limit_bytes=24 * MIB),
        name="resample",
    )(ids, latent_param, features, away(hidden), *[away(w) for w in weights])


def resample_own_kernel(ids, lat, feat, *rest):
    weights, out, held, frame, work, sems = (
        rest[:4],
        rest[4],
        rest[5:9],
        rest[9],
        rest[10:-1],
        rest[-1],
    )
    qp, kp, vp, op = held
    loads = [pltpu.make_async_copy(a, b, sems.at[i]) for i, (a, b) in enumerate(zip(weights, held))]
    loads.append(pltpu.make_async_copy(feat.at[ids[0]], frame, sems.at[4]))
    for load in loads:
        load.start()
    for load in loads[:3]:
        load.wait()
    prepare(lat, qp, kp, vp, *work)
    for load in loads[3:]:
        load.wait()
    out[...] = one_image(frame, kp, vp, op, *work)


def resample_own(ids, features, latent_param, weights):
    _, patches, vdim = features.shape
    inner = weights[0].shape[1]
    return pl.pallas_call(
        resample_own_kernel,
        out_shape=pltpu.VMEM((LATENTS, vdim), F32),
        in_specs=[IN_SMEM, IN_VMEM] + [IN_HBM] * 5,
        out_specs=IN_VMEM,
        scratch_shapes=[pltpu.VMEM(w.shape, BF16) for w in weights]
        + [pltpu.VMEM((patches, vdim), BF16)]
        + resample_scratch(patches, vdim, inner)
        + [pltpu.SemaphoreType.DMA((5,))],
        compiler_params=pltpu.CompilerParams(vmem_limit_bytes=20 * MIB),
        name="resample",
    )(ids, latent_param, features, *[away(w) for w in weights])


def combine_kernel(lat, squares, own, a, b, c, out, total_squares):
    total = own[...]
    sums = squares[...]
    count = squares.shape[0]
    for part in (a, b, c):
        total = total + part[:LATENTS, :].astype(F32)
        line = part[LATENTS:, :].astype(F32)[0:1, :]
        at = lambda i: line[:, i * 128 : (i + 1) * 128]
        sums = sums + jnp.concatenate([at(i) + at(count + i) for i in range(count)], axis=0)
    out[...] = normalize(lat[...].astype(F32) + total).astype(BF16)
    total_squares[...] = sums


def combine(latent_param, squares, own, parts):
    return pl.pallas_call(
        combine_kernel,
        out_shape=[
            pltpu.VMEM(latent_param.shape, BF16),
            pltpu.VMEM(squares.shape, F32),
        ],
        in_specs=[IN_VMEM] * 6,
        out_specs=[IN_VMEM] * 2,
        compiler_params=pltpu.CompilerParams(vmem_limit_bytes=8 * MIB),
        name="combine",
    )(latent_param, squares, near(own), *[near(p) for p in parts])


TILE = 512
AHEAD = 3


def project_kernel(count, moved, flags, *refs):
    chunks, refs = refs[:count], refs[count:]
    hid, own_k, own_v, other_k, other_v = refs[:5]
    keys, vals, far_keys, far_vals = refs[5:9]
    near_hid = refs[9 : 9 + moved]
    chosen, tiles, sems, out_sems, hid_sems = refs[9 + moved :]
    width = keys.shape[1]
    steps = 2 * (width // TILE)

    def fetch(step):
        cols = pl.ds(pl.multiple_of(step // 2 * TILE, TILE), TILE)

        def one(src):
            return pltpu.make_async_copy(src.at[0, :, cols], tiles.at[step], sems.at[step])

        return one

    def start(step, of_own, of_other):
        @pl.when(flags[0] == 0)
        def _():
            fetch(step)(of_own).start()

        @pl.when(flags[0] != 0)
        def _():
            fetch(step)(of_other).start()

    for step in range(AHEAD):
        start(step, *((own_v, other_v) if step % 2 else (own_k, other_k)))
    loads = [
        pltpu.make_async_copy(hid.at[flags[1 + i]], near_hid[i], hid_sems.at[i])
        for i in range(moved)
    ]
    for i, a in enumerate(chunks):
        chosen[i * LATENTS : (i + 1) * LATENTS, :] = a[...]

    def store(step, src, dst):
        cols = pl.ds(pl.multiple_of(step // 2 * TILE, TILE), TILE)
        return pltpu.make_async_copy(src.at[:, cols], dst.at[:, cols], out_sems.at[step])

    def column(j, carry):
        cols = pl.ds(pl.multiple_of(j * TILE, TILE), TILE)
        for i, (out, far) in enumerate(((keys, far_keys), (vals, far_vals))):
            step = 2 * j + i
            fetch(step)(own_k).wait()

            @pl.when(step + AHEAD < steps)
            def _():
                if (i + AHEAD) % 2:
                    start(step + AHEAD, own_v, other_v)
                else:
                    start(step + AHEAD, own_k, other_k)

            out[:, cols] = dot(chosen[...], tiles[step]).astype(BF16)
            store(step, out, far).start()
        return carry

    lax.fori_loop(0, steps // 2, column, 0)
    for load in loads:
        load.start()
    for step in range(steps):
        store(step, keys, far_keys).wait()
    for load in loads:
        load.wait()


def project(flags, chunks, own, other, hidden, moved):
    vdim, width = own[0].shape[1:]
    rows = len(chunks) * LATENTS
    steps = 2 * (width // TILE)
    return pl.pallas_call(
        functools.partial(project_kernel, len(chunks), moved),
        out_shape=[pltpu.VMEM((rows, width), BF16)] * 2
        + [pltpu.HBM((rows, width), BF16)] * 2
        + [pltpu.VMEM(hidden.shape[1:], BF16)] * moved,
        in_specs=[IN_SMEM] + [IN_VMEM] * len(chunks) + [IN_HBM] * 5,
        out_specs=[IN_VMEM] * 2 + [IN_HBM] * 2 + [IN_VMEM] * moved,
        scratch_shapes=[
            pltpu.VMEM((rows, vdim), BF16),
            pltpu.VMEM((steps, vdim, TILE), BF16),
            pltpu.SemaphoreType.DMA((steps,)),
            pltpu.SemaphoreType.DMA((steps,)),
            pltpu.SemaphoreType.DMA((2,)),
        ],
        compiler_params=pltpu.CompilerParams(vmem_limit_bytes=24 * MIB),
        cost_estimate=pl.CostEstimate(
            flops=4 * rows * vdim * width, bytes_accessed=0, transcendentals=0
        ),
        name="project",
    )(flags, *[near(a) for a in chunks], *[away(a) for a in (hidden, *own, *other)])


def layer_kernel(row, places, count, ahead, streamed, *refs):
    batches = len(places)
    xs, metas, refs = refs[:batches], refs[batches : 2 * batches], refs[2 * batches :]
    keys, vals, refs = refs[0], refs[1], refs[2:]
    squares, before, refs = refs[:count], refs[count : count + ahead], refs[count + ahead :]
    ys, square_out, refs = refs[:batches], refs[batches], refs[batches + 1 :]
    scale_s, bias_s, high_s, half_s, gate_s, acc = refs[:6]
    rows = xs[0].shape[0]
    heads = xs[0].shape[1] // HEAD
    slots = 4 * LATENTS
    loads = []
    if streamed:
        near_keys, near_vals, sems = refs[6:]
        for i, (at, _) in enumerate(places):
            loads.append(
                [
                    pltpu.make_async_copy(
                        src.at[pl.ds(at * slots, slots)], dst.at[i], sems.at[i, j]
                    )
                    for j, (src, dst) in enumerate(((keys, near_keys), (vals, near_vals)))
                ]
            )
        for load in loads[0]:
            load.start()

    total = squares[0][...]
    for part in squares[1:]:
        total = total + part[...]
    ones = jnp.ones((slots, HEAD), BF16)
    lines = [b[...] for b in before]
    for i, (at, line) in enumerate(places):
        scale = lax.rsqrt(total[line : line + 1, :] / D + EPS) * (HEAD ** (-0.5) * LOG2E)
        spare = jnp.zeros((rows - 3, rows), F32)
        gate = metas[i][row : row + 1, :]
        cols = jnp.concatenate([scale, metas[i][0:1, :], gate, spare], axis=0).T
        slot = jnp.broadcast_to(cols[:, 1:2], (rows, HEAD))
        scale_s[...] = jnp.broadcast_to(cols[:, 0:1], (rows, HEAD))
        gate_s[...] = jnp.broadcast_to(cols[:, 2:3], (rows, HEAD))
        upper = jnp.where(slot > 1.5, 1.0, 0.0)
        high_s[...] = upper
        half_s[...] = upper.astype(BF16)
        half = (lax.broadcasted_iota(jnp.int32, (rows, HEAD), 1) // LATENTS).astype(F32)
        bias_s[...] = jnp.where(slot - 2.0 * upper == half, 0.0, NEG)
        high = high_s[...] > 0.5
        if streamed:
            for load in loads[i]:
                load.wait()
            for load in loads[i + 1] if i + 1 < batches else ():
                load.start()
        sums = jnp.zeros((rows, HEAD), F32)
        for h in range(heads):
            cols = slice(h * HEAD, (h + 1) * HEAD)
            if streamed:
                k, v = near_keys[i, :, cols], near_vals[i, :, cols]
            else:
                k = keys[at * slots : (at + 1) * slots, cols]
                v = vals[at * slots : (at + 1) * slots, cols]
            q = xs[i][:, cols]
            score = dot_nt(q, k)
            t = jnp.where(high, score[:, HEAD:], score[:, :HEAD]) * scale_s[...] + bias_s[...]
            e = jnp.exp2(t - jnp.max(t, axis=1, keepdims=True)).astype(BF16)
            e_high = e * half_s[...]
            weight = jnp.concatenate([e - e_high, e_high], axis=1)
            mixed = dot(weight, jnp.concatenate([v, ones], axis=1))
            attn = mixed[:, :HEAD] / mixed[:, HEAD:]
            out = (q.astype(F32) + gate_s[...] * attn).astype(BF16)
            ys[i][:, cols] = out
            of = out.astype(F32)
            sums = sums + of * of
        acc[...] = sums
        lines.append(jnp.sum(acc[...].T, axis=0, keepdims=True))
    square_out[...] = jnp.concatenate(lines, axis=0)


def layer(row, xs, metas, kv, places, squares, before=(), streamed=False):
    keys, vals = kv
    rows, width = xs[0].shape
    slots = 4 * LATENTS
    batches = len(xs)
    scratch = pltpu.VMEM((rows, HEAD), F32)
    place = away if streamed else near
    where = IN_HBM if streamed else IN_VMEM
    extra = [pltpu.VMEM((batches, slots, width), BF16)] * 2 + [pltpu.SemaphoreType.DMA((batches, 2))]
    return pl.pallas_call(
        functools.partial(layer_kernel, row, places, len(squares), len(before), streamed),
        out_shape=[pltpu.VMEM((rows, width), BF16)] * batches
        + [pltpu.VMEM((batches + len(before), rows), F32)],
        in_specs=[IN_VMEM] * (2 * batches)
        + [where, where]
        + [IN_VMEM] * (len(squares) + len(before)),
        out_specs=[IN_VMEM] * (batches + 1),
        scratch_shapes=[scratch] * 3
        + [pltpu.VMEM((rows, HEAD), BF16)]
        + [scratch] * 2
        + (extra if streamed else []),
        compiler_params=pltpu.CompilerParams(vmem_limit_bytes=12 * MIB),
        cost_estimate=pl.CostEstimate(
            flops=16 * batches * rows * slots * width,
            bytes_accessed=0,
            transcendentals=batches * rows * width,
        ),
        name="layer",
    )(
        *[near(x) for x in xs],
        *metas,
        place(keys),
        place(vals),
        *[near(a) for a in squares],
        *[near(a) for a in before],
    )


def body(
    features,
    latent_param,
    query_proj,
    key_proj,
    value_proj,
    out_proj,
    hidden,
    key_weight,
    value_weight,
    gate_angle,
    group_images,
    token_slot,
    attend,
):
    s = lax.axis_index("section")
    c = lax.axis_index("seq")
    m = lax.axis_index("mp")
    core = s & 1
    far = s >> 1
    mates = lax.axis_size("mp")
    seqs = lax.axis_size("seq")
    sections = lax.axis_size("section")

    def mp_shift(a, k):
        return lax.ppermute(a, "mp", [(i, (i + k) % mates) for i in range(mates)])

    def core_swap(a):
        return lax.ppermute(a, "section", [(i, i ^ 1) for i in range(sections)])

    def far_swap(a):
        return lax.ppermute(a, "section", [(i, i ^ 2) for i in range(sections)])

    def cross(a):
        return lax.ppermute(a, "section", [(0, 2), (1, 3)])

    def spread(a):
        return [a] + [mp_shift(a, k) for k in (1, 2, 3)]

    other_w = (core_swap(key_weight), core_swap(value_weight))
    gate_own = jnp.broadcast_to(jnp.tanh(gate_angle)[:, None], (1, 128))
    gate_other = core_swap(gate_own)
    gate_first = jnp.where(core == 0, gate_own, gate_other)
    gate_second = jnp.where(core == 0, gate_other, gate_own)

    order = jnp.stack([(m + 2) & 3, (m + 1) & 3, (m + 3) & 3, core]).astype(jnp.int32)
    weights = (query_proj, key_proj, value_proj, out_proj)
    p2, p1, p3, squares = resample_sent(order, features, latent_param, hidden, weights)
    r2, r1, r3 = mp_shift(p2, 2), mp_shift(p1, 1), mp_shift(p3, 3)
    p0 = resample_own(m[None].astype(jnp.int32), features, latent_param, weights)
    latents, entering = combine(latent_param, squares, p0, (r1, r2, r3))

    left = lax.ppermute(latents, "seq", [(i, i + 1) for i in range(seqs - 1)])
    right = lax.ppermute(latents, "seq", [(i + 1, i) for i in range(seqs - 1)])
    firsts = group_images[:, 0, 0]
    start = lax.dynamic_index_in_dim(firsts, s, 0, keepdims=False)
    where_is = ((start + ((m - start) & 3)) >> 2) - c
    picked = jnp.where(where_is == 0, latents, jnp.where(where_is < 0, left, right))
    chosen = spread(picked) + spread(far_swap(picked))

    block = (m - firsts[:, None] - token_slot[:, 0, :]) & 3
    alive = attend[:, 0, :].astype(F32)
    rows = jnp.stack(
        [block.astype(F32), alive * gate_first, alive * gate_second]
        + [jnp.zeros_like(alive)] * 5,
        axis=1,
    )
    meta_own = lax.dynamic_index_in_dim(rows, s, 0, keepdims=False)
    meta_far = lax.dynamic_index_in_dim(rows, s ^ 2, 0, keepdims=False)

    own_w = (key_weight, value_weight)
    flags_first = jnp.stack([core, core, core + 2]).astype(jnp.int32)
    flags_second = jnp.stack([1 - core, core, core + 2]).astype(jnp.int32)
    k, v, k_away, v_away, hidden0, hidden1 = project(
        flags_first, chosen, own_w, other_w, hidden, 2
    )
    first, first_away = (k, v), (k_away, v_away)
    k, v, k_away, v_away = project(flags_second, chosen, own_w, other_w, hidden, 0)
    second, second_away = (k, v), (k_away, v_away)

    metas = [meta_own, meta_far]
    a0, a1, qa = layer(1, [hidden0, hidden1], metas, first, ((0, 0), (1, 1)), [entering])
    qa = spread(qa)
    b0, qb0 = layer(2, [a0], [meta_own], second, ((0, 0),), qa)
    x0 = cross(b0)
    b1, qb = layer(2, [a1], [meta_far], second, ((1, 1),), qa, [qb0])
    x1 = cross(b1)
    qb = cross(sum(spread(qb)))

    metas = [meta_far, meta_own]
    turned = ((1, 0), (0, 1))
    c0, c1, qc = layer(1, [x0, x1], metas, first_away, turned, [qb], streamed=True)
    qc = spread(qc)
    d0, d1, _ = layer(2, [c0, c1], metas, second_away, turned, qc, streamed=True)

    def split(a, b, c_, d_):
        first = jnp.where(far == 0, a, c_)
        second = jnp.where(far == 0, b, d_)
        keep = jnp.where(core == 0, first, second)
        send = jnp.where(core == 0, second, first)
        return keep, core_swap(send)

    keep0, got0 = split(a0, b0, c0, d0)
    keep1, got1 = split(a1, b1, c1, d1)
    even = core == 0
    return jnp.stack(
        [
            jnp.where(even, keep0, got0),
            jnp.where(even, got0, keep0),
            jnp.where(even, keep1, got1),
            jnp.where(even, got1, keep1),
        ]
    )[None]


def solution(mesh):
    return jax.shard_map(
        body,
        mesh=mesh,
        in_specs=(
            P(("section", "seq"), None, None),
            P(),
            P(None, "mp"),
            P(None, "mp"),
            P(None, "mp"),
            P("mp", None),
            P(None, "seq", "mp"),
            P("section", None, "mp"),
            P("section", None, "mp"),
            P("section"),
            P(None, "seq", None),
            P(None, "seq", None),
            P(None, "seq", None),
        ),
        out_specs=P("section", None, "seq", "mp"),
        check_vma=False,
    )
```

```python
import functools

import jax
import jax.numpy as jnp
from jax import lax
from jax.experimental import pallas as pl
from jax.experimental.pallas import tpu as pltpu
from jax.sharding import PartitionSpec as P

D = 8192
HEAD = 128
LATENTS = 64
PHEAD = 96
EPS = 1e-05
NEG = -1e30
LOG2E = 1.4426950408889634
F32 = jnp.float32
BF16 = jnp.bfloat16
MIB = 1024 * 1024
FEW = 1000
SPARE = 16


def normalize(v):
    mean = jnp.mean(v, axis=-1, keepdims=True)
    cent = v - mean
    var = jnp.mean(cent * cent, axis=-1, keepdims=True)
    return cent * lax.rsqrt(var + EPS)


def dot(a, b):
    return jnp.dot(a, b, preferred_element_type=F32)


def dot_nt(a, b):
    return lax.dot_general(a, b, (((1,), (1,)), ((), ())), preferred_element_type=F32)


def up16(n):
    return -(-n // 16) * 16


def up128(n):
    return -(-n // 128) * 128


def near(a):
    return pltpu.with_memory_space_constraint(a, pltpu.VMEM)


def away(a):
    return pltpu.with_memory_space_constraint(a, pltpu.HBM)


IN_VMEM = pl.BlockSpec(memory_space=pltpu.VMEM)
IN_SMEM = pl.BlockSpec(memory_space=pltpu.SMEM)
IN_HBM = pl.BlockSpec(memory_space=pltpu.HBM)


def resample_updates(frames, lat, weights, held, ctx, tail, pk, pv, pqm, mixed, sems):
    n = len(frames)
    patches = frames[0].shape[0]
    keys = LATENTS + patches
    rows = up16(keys)
    qp, kp, vp, op = held
    inner = qp.shape[1]
    heads = inner // PHEAD
    cut = inner // 256 * 256
    side = inner - cut
    loads = [pltpu.make_async_copy(a, b, sems.at[i]) for i, (a, b) in enumerate(zip(weights, held))]
    for i in (1, 2, 0, 3):
        loads[i].start()

    base = normalize(lat[...].astype(F32)).astype(BF16)
    for i in range(n):
        top = i * rows
        ctx[top : top + LATENTS, :] = base
        ctx[top + rows - 16 : top + rows, :] = jnp.zeros((16, ctx.shape[1]), BF16)
        for r in range(0, patches, 64):
            end = min(r + 64, patches)
            block = normalize(frames[i][r:end, :].astype(F32)).astype(BF16)
            ctx[top + LATENTS + r : top + LATENTS + end, :] = block
    pv[:, inner:] = jnp.ones((pv.shape[0], 128), BF16)

    for i in (1, 2):
        loads[i].wait()
    tail[:, :side] = kp[:, cut:]
    tail[:, side:] = vp[:, cut:]
    pk[:, :cut] = dot(ctx[...], kp[:, :cut]).astype(BF16)
    pv[:, :cut] = dot(ctx[...], vp[:, :cut]).astype(BF16)
    both = dot(ctx[...], tail[...]).astype(BF16)
    pk[:, cut:] = both[:, :side]
    pv[:, cut:inner] = both[:, side:]
    loads[0].wait()
    pq = dot(base, qp[...]).astype(BF16).astype(F32)
    which = lax.broadcasted_iota(jnp.int32, (LATENTS, inner), 1) // PHEAD
    for h in range(heads):
        pqm[h * LATENTS : (h + 1) * LATENTS, :] = jnp.where(which == h, pq, 0.0).astype(BF16)

    for i in range(n):
        own = slice(i * rows, (i + 1) * rows)
        score = dot_nt(pqm[...], pk[own, :]) * (PHEAD ** (-0.5) * LOG2E)
        lane = lax.broadcasted_iota(jnp.int32, score.shape, 1)
        score = jnp.where(lane < keys, score, NEG)
        e = jnp.exp2(score - jnp.max(score, axis=1, keepdims=True)).astype(BF16)
        mix = dot(e, pv[own, :])
        inverse = 1.0 / mix[:, inner:]
        for j in range(inner // 128):
            at = lax.broadcasted_iota(jnp.int32, (LATENTS, 128), 1) + j * 128
            tile = jnp.zeros((LATENTS, 128), F32)
            for h in range(j * 128 // PHEAD, (j * 128 + 127) // PHEAD + 1):
                rows_h = slice(h * LATENTS, (h + 1) * LATENTS)
                value = mix[rows_h, j * 128 : (j + 1) * 128] * inverse[rows_h, :]
                tile = jnp.where(at // PHEAD == h, value, tile)
            mixed[i * LATENTS : (i + 1) * LATENTS, j * 128 : (j + 1) * 128] = tile.astype(BF16)
    loads[3].wait()
    return dot(mixed[...], op[...])


def resample_scratch(n, patches, vdim, inner, weights):
    rows = n * up16(LATENTS + patches)
    cut = inner // 256 * 256
    return [pltpu.VMEM(w.shape, BF16) for w in weights] + [
        pltpu.VMEM((rows, vdim), BF16),
        pltpu.VMEM((vdim, 2 * (inner - cut)), BF16),
        pltpu.VMEM((rows, inner), BF16),
        pltpu.VMEM((rows, inner + 128), BF16),
        pltpu.VMEM((inner // PHEAD * LATENTS, inner), BF16),
        pltpu.VMEM((n * LATENTS, inner), BF16),
        pltpu.SemaphoreType.DMA((4,)),
    ]


def resample_sent_kernel(n, ids, lat, feat, hid, *refs):
    weights, sent, squares, refs = refs[:4], refs[4 : 4 + n], refs[4 + n], refs[5 + n :]
    near_hid, hid_sems = refs[0:2], refs[2]
    loads = [
        pltpu.make_async_copy(hid.at[ids[n + i]], near_hid[i], hid_sems.at[i]) for i in range(2)
    ]
    frames = [feat.at[ids[i]] for i in range(n)]
    update = resample_updates(frames, lat, weights, refs[3:7], *refs[7:])
    for load in loads:
        load.start()
    for i in range(n):
        sent[i][0:LATENTS, :] = update[i * LATENTS : (i + 1) * LATENTS].astype(BF16)
    lines = []
    for load, a in zip(loads, near_hid):
        load.wait()
        acc = jnp.zeros((a.shape[0], 128), F32)
        for at in range(0, a.shape[1], 128):
            v = a[:, at : at + 128].astype(F32)
            acc = acc + v * v
        lines.append(jnp.sum(acc.T, axis=0, keepdims=True))
    squares[...] = jnp.concatenate(lines, axis=0)
    line = as_line(lines, sent[0].shape[1])
    for i in range(n):
        sent[i][LATENTS:, :] = line


def resample_sent(ids, features, latent_param, hidden, weights):
    n = ids.shape[0] - 2
    _, patches, vdim = features.shape
    _, rows, width = hidden.shape
    inner = weights[0].shape[1]
    return pl.pallas_call(
        functools.partial(resample_sent_kernel, n),
        out_shape=[pltpu.VMEM((LATENTS + SPARE, vdim), BF16)] * n
        + [pltpu.VMEM((2, rows), F32)],
        in_specs=[IN_SMEM, IN_VMEM, IN_VMEM] + [IN_HBM] * 5,
        out_specs=[IN_VMEM] * (n + 1),
        scratch_shapes=[pltpu.VMEM((rows, width), BF16)] * 2
        + [pltpu.SemaphoreType.DMA((2,))]
        + resample_scratch(n, patches, vdim, inner, weights),
        compiler_params=pltpu.CompilerParams(vmem_limit_bytes=24 * MIB),
        name="resample",
    )(ids, latent_param, near(features), away(hidden), *[away(w) for w in weights])


def resample_own_kernel(ids, lat, feat, *refs):
    refs[4][...] = resample_updates([feat.at[ids[0]]], lat, refs[:4], refs[5:9], *refs[9:])


def resample_own(ids, features, latent_param, weights):
    _, patches, vdim = features.shape
    inner = weights[0].shape[1]
    return pl.pallas_call(
        resample_own_kernel,
        out_shape=pltpu.VMEM((LATENTS, vdim), F32),
        in_specs=[IN_SMEM, IN_VMEM, IN_VMEM] + [IN_HBM] * 4,
        out_specs=IN_VMEM,
        scratch_shapes=resample_scratch(1, patches, vdim, inner, weights),
        compiler_params=pltpu.CompilerParams(vmem_limit_bytes=16 * MIB),
        name="resample",
    )(ids, latent_param, near(features), *[away(w) for w in weights])


def combine_kernel(lat, squares, own, a, b, c, out, total_squares):
    total = own[...]
    sums = squares[...]
    count = squares.shape[0]
    for part in (a, b, c):
        total = total + part[:LATENTS, :].astype(F32)
        line = part[LATENTS:, :].astype(F32)[0:1, :]
        at = lambda i: line[:, i * 128 : (i + 1) * 128]
        sums = sums + jnp.concatenate([at(i) + at(count + i) for i in range(count)], axis=0)
    out[...] = normalize(lat[...].astype(F32) + total).astype(BF16)
    total_squares[...] = sums


def combine(latent_param, squares, own, parts):
    return pl.pallas_call(
        combine_kernel,
        out_shape=[
            pltpu.VMEM(latent_param.shape, BF16),
            pltpu.VMEM(squares.shape, F32),
        ],
        in_specs=[IN_VMEM] * 6,
        out_specs=[IN_VMEM] * 2,
        compiler_params=pltpu.CompilerParams(vmem_limit_bytes=8 * MIB),
        name="combine",
    )(latent_param, squares, near(own), *[near(p) for p in parts])


TILE = 512
AHEAD = 3


def project_kernel(count, moved, flags, *refs):
    chunks, refs = refs[:count], refs[count:]
    hid, own_k, own_v, other_k, other_v = refs[:5]
    keys, vals, tiles = refs[5:8]
    near_hid = refs[8 : 8 + moved]
    chosen, sems, hid_sems = refs[8 + moved :]
    steps = 2 * (keys.shape[1] // TILE)

    def fetch(step, src):
        cols = pl.ds(pl.multiple_of(step // 2 * TILE, TILE), TILE)
        return pltpu.make_async_copy(src.at[0, :, cols], tiles.at[step], sems.at[step])

    def start(step, odd):
        of_own, of_other = (own_v, other_v) if odd else (own_k, other_k)

        @pl.when(flags[0] == 0)
        def _():
            fetch(step, of_own).start()

        @pl.when(flags[0] != 0)
        def _():
            fetch(step, of_other).start()

    @pl.when(flags[1] != 0)
    def _():
        for step in range(AHEAD):
            start(step, step % 2)
        loads = [
            pltpu.make_async_copy(hid.at[flags[2 + i]], near_hid[i], hid_sems.at[i])
            for i in range(moved)
        ]
        for load in loads:
            load.start()
        top = 0
        for a in chunks:
            chosen[top : top + a.shape[0], :] = a[...]
            top += a.shape[0]

        def column(j, carry):
            cols = pl.ds(pl.multiple_of(j * TILE, TILE), TILE)
            for i, out in enumerate((keys, vals)):
                step = 2 * j + i
                fetch(step, own_k).wait()

                @pl.when(step + AHEAD < steps)
                def _():
                    start(step + AHEAD, (i + AHEAD) % 2)

                out[:, cols] = dot(chosen[...], tiles[step]).astype(BF16)
            return carry

        lax.fori_loop(0, steps // 2, column, 0)
        for load in loads:
            load.wait()


def project(flags, chunks, own, other, hidden, moved=0, keep=False):
    vdim, width = own[0].shape[1:]
    rows = sum(a.shape[0] for a in chunks)
    steps = 2 * (width // TILE)
    held = pltpu.VMEM((steps, vdim, TILE), BF16)
    kernel = functools.partial(project_kernel, len(chunks), moved)
    if not keep:
        inner = kernel

        def kernel(*refs):
            at = 1 + len(chunks) + 7
            refs, tiles = refs[:-1], refs[-1]
            return inner(*refs[:at], tiles, *refs[at:])

    return pl.pallas_call(
        kernel,
        out_shape=[pltpu.VMEM((rows, width), BF16)] * 2
        + [held] * keep
        + [pltpu.VMEM(hidden.shape[1:], BF16)] * moved,
        in_specs=[IN_SMEM] + [IN_VMEM] * len(chunks) + [IN_HBM] * 5,
        out_specs=[IN_VMEM] * (2 + keep + moved),
        scratch_shapes=[
            pltpu.VMEM((rows, vdim), BF16),
            pltpu.SemaphoreType.DMA((steps,)),
            pltpu.SemaphoreType.DMA((2,)),
        ]
        + [held] * (not keep),
        compiler_params=pltpu.CompilerParams(vmem_limit_bytes=(8 if keep else 20) * MIB),
        cost_estimate=pl.CostEstimate(
            flops=FEW, bytes_accessed=0, transcendentals=0
        ),
        name="project",
    )(flags, *[near(a) for a in chunks], *[away(a) for a in (hidden, *own, *other)])


def project_both_kernel(flags, a, b, own_k, own_v, other_k, other_v, k1, v1, k2, v2, chosen, ring, sems):
    part = a.shape[0]
    half = 2 * (k1.shape[1] // TILE)
    depth = ring.shape[0]

    def fetch(step, src):
        cols = pl.ds(pl.multiple_of(step % half // 2 * TILE, TILE), TILE)
        return pltpu.make_async_copy(src.at[0, :, cols], ring.at[step % depth], sems.at[step % depth])

    def start(step, odd):
        of_own, of_other = (own_v, other_v) if odd else (own_k, other_k)
        from_own = (step // half) == flags[0]

        @pl.when(from_own)
        def _():
            fetch(step, of_own).start()

        @pl.when(jnp.logical_not(from_own))
        def _():
            fetch(step, of_other).start()

    @pl.when(flags[1] != 0)
    def _():
        for step in range(depth - 1):
            start(step, step % 2)
        chosen[0:part, :] = a[...]
        chosen[part:, :] = b[...]
        for which, outs in enumerate(((k1, v1), (k2, v2))):

            def column(j, carry, which=which, outs=outs):
                cols = pl.ds(pl.multiple_of(j * TILE, TILE), TILE)
                for i, out in enumerate(outs):
                    step = which * half + 2 * j + i
                    fetch(step, own_k).wait()

                    @pl.when(step + depth - 1 < 2 * half)
                    def _():
                        start(step + depth - 1, (i + depth - 1) % 2)

                    out[:, cols] = dot(chosen[...], ring[step % depth]).astype(BF16)
                return carry

            lax.fori_loop(0, half // 2, column, 0)


def project_both(flags, a, b, own, other):
    vdim, width = own[0].shape[1:]
    rows = a.shape[0] + b.shape[0]
    return pl.pallas_call(
        project_both_kernel,
        out_shape=[pltpu.VMEM((rows, width), BF16)] * 4,
        in_specs=[IN_SMEM, IN_VMEM, IN_VMEM] + [IN_HBM] * 4,
        out_specs=[IN_VMEM] * 4,
        scratch_shapes=[
            pltpu.VMEM((rows, vdim), BF16),
            pltpu.VMEM((AHEAD + 1, vdim, TILE), BF16),
            pltpu.SemaphoreType.DMA((AHEAD + 1,)),
        ],
        compiler_params=pltpu.CompilerParams(vmem_limit_bytes=16 * MIB),
        cost_estimate=pl.CostEstimate(flops=FEW, bytes_accessed=0, transcendentals=0),
        name="project",
    )(flags, near(a), near(b), *[away(w) for w in (*own, *other)])


def project_held_kernel(flags, a, tiles, *refs):
    keys, vals = refs[-2:]

    @pl.when(flags[1] != 0)
    def _():
        def column(j, carry):
            cols = pl.ds(pl.multiple_of(j * TILE, TILE), TILE)
            keys[:, cols] = dot(a[...], tiles[2 * j]).astype(BF16)
            vals[:, cols] = dot(a[...], tiles[2 * j + 1]).astype(BF16)
            return carry

        lax.fori_loop(0, keys.shape[1] // TILE, column, 0)


def project_held(flags, a, tiles, after=()):
    steps, vdim, _ = tiles.shape
    rows = a.shape[0]
    width = steps // 2 * TILE
    return pl.pallas_call(
        project_held_kernel,
        out_shape=[pltpu.VMEM((rows, width), BF16)] * 2,
        in_specs=[IN_SMEM] + [IN_VMEM] * (2 + len(after)),
        out_specs=[IN_VMEM] * 2,
        compiler_params=pltpu.CompilerParams(vmem_limit_bytes=8 * MIB),
        cost_estimate=pl.CostEstimate(
            flops=FEW, bytes_accessed=0, transcendentals=0
        ),
        name="project",
    )(flags, near(a), near(tiles), *[near(b) for b in after])


def gather_kernel(*refs):
    for i, a in enumerate(refs[:-1]):
        refs[-1][i * LATENTS : (i + 1) * LATENTS, :] = a[...]


def gather(chunks):
    vdim = chunks[0].shape[1]
    return pl.pallas_call(
        gather_kernel,
        out_shape=pltpu.VMEM((len(chunks) * LATENTS, vdim), BF16),
        in_specs=[IN_VMEM] * len(chunks),
        out_specs=IN_VMEM,
        compiler_params=pltpu.CompilerParams(vmem_limit_bytes=2 * MIB),
        name="gather",
    )(*[near(a) for a in chunks])


def as_line(lines, width):
    high = [line.astype(BF16).astype(F32) for line in lines]
    low = [line - h for line, h in zip(lines, high)]
    parts = high + low
    spare = jnp.zeros((1, width - len(parts) * parts[0].shape[1]), F32)
    line = jnp.concatenate(parts + [spare], axis=1)
    first = lax.broadcasted_iota(jnp.int32, (SPARE, width), 0) == 0
    return jnp.where(first, line, 0.0).astype(BF16)


def from_line_kernel(x, *refs):
    out = refs[-1]
    line = x[x.shape[0] - SPARE :, :].astype(F32)[0:1, :]
    at = lambda i: line[:, i * 128 : (i + 1) * 128]
    count = out.shape[0]
    out[...] = jnp.concatenate([at(i) + at(count + i) for i in range(count)], axis=0)


def from_line(x, after):
    return pl.pallas_call(
        from_line_kernel,
        out_shape=pltpu.VMEM((1, 128), F32),
        in_specs=[IN_VMEM] * (1 + len(after)),
        out_specs=IN_VMEM,
        compiler_params=pltpu.CompilerParams(vmem_limit_bytes=2 * MIB),
        name="from_line",
    )(near(x), *[near(a) for a in after])


def layer_kernel(row, places, count, ahead, riding, others, routed, carried, *refs):
    batches = len(places)
    flags, refs = (refs[0], refs[1:]) if others else (None, refs)
    xs, metas, refs = refs[:batches], refs[batches : 2 * batches], refs[2 * batches :]
    keys, vals, refs = refs[0], refs[1], refs[2:]
    squares, before, refs = refs[:count], refs[count : count + ahead], refs[count + ahead :]
    alts, refs = refs[:others], refs[others + carried :]
    outs, refs = refs[: batches * (1 + routed)], refs[batches * (1 + routed) :]
    square_out, refs = refs[0], refs[1 + carried :]
    scale_s, bias_s, high_s, half_s, gate_s, acc = refs
    rows = metas[0].shape[1]
    heads = xs[0].shape[1] // HEAD
    slots = 4 * LATENTS

    def write(i, cols, old, new):
        if routed:
            outs[2 * i][:, cols] = jnp.where(flags[1] == 0, old, new)
            outs[2 * i + 1][:, cols] = jnp.where(flags[1] == 0, new, old)
        else:
            outs[i][0:rows, cols] = new

    def run():
        total = squares[0][...]
        for part in squares[1:]:
            total = total + part[...]
        ones = jnp.ones((slots, HEAD), BF16)
        lines = [b[...] for b in before]
        for i, (at, line) in enumerate(places):
            scale = lax.rsqrt(total[line : line + 1, :] / D + EPS) * (HEAD ** (-0.5) * LOG2E)
            spare = jnp.zeros((rows - 3, rows), F32)
            gate = metas[i][row : row + 1, :]
            cols = jnp.concatenate([scale, metas[i][0:1, :], gate, spare], axis=0).T
            slot = jnp.broadcast_to(cols[:, 1:2], (rows, HEAD))
            scale_s[...] = jnp.broadcast_to(cols[:, 0:1], (rows, HEAD))
            gate_s[...] = jnp.broadcast_to(cols[:, 2:3], (rows, HEAD))
            upper = jnp.where(slot > 1.5, 1.0, 0.0)
            high_s[...] = upper
            half_s[...] = upper.astype(BF16)
            half = (lax.broadcasted_iota(jnp.int32, (rows, HEAD), 1) // LATENTS).astype(F32)
            bias_s[...] = jnp.where(slot - 2.0 * upper == half, 0.0, NEG)
            high = high_s[...] > 0.5
            sums = jnp.zeros((rows, HEAD), F32)
            for h in range(heads):
                cols = slice(h * HEAD, (h + 1) * HEAD)
                k = keys[at * slots : (at + 1) * slots, cols]
                v = vals[at * slots : (at + 1) * slots, cols]
                q = xs[i][0:rows, cols]
                score = dot_nt(q, k)
                t = jnp.where(high, score[:, HEAD:], score[:, :HEAD]) * scale_s[...] + bias_s[...]
                e = jnp.exp2(t - jnp.max(t, axis=1, keepdims=True)).astype(BF16)
                e_high = e * half_s[...]
                weight = jnp.concatenate([e - e_high, e_high], axis=1)
                mixed = dot(weight, jnp.concatenate([v, ones], axis=1))
                attn = mixed[:, :HEAD] / mixed[:, HEAD:]
                out = (q.astype(F32) + gate_s[...] * attn).astype(BF16)
                write(i, cols, q, out)
                of = out.astype(F32)
                sums = sums + of * of
            acc[...] = sums
            lines.append(jnp.sum(acc[...].T, axis=0, keepdims=True))
        square_out[...] = jnp.concatenate(lines, axis=0)
        if riding:
            outs[-1][rows:, :] = as_line(lines, outs[-1].shape[1])

    if not others:
        run()
        return
    pl.when(flags[0] != 0)(run)

    @pl.when(flags[0] == 0)
    def _():
        for i in range(batches):
            for h in range(heads):
                cols = slice(h * HEAD, (h + 1) * HEAD)
                write(i, cols, alts[i][0:rows, cols], alts[batches + i][0:rows, cols])
        square_out[...] = jnp.zeros_like(square_out)


def layer(
    row, xs, metas, kv, places, squares, before=(), riding=False, flags=None, alts=(), routed=False, carry=()
):
    keys, vals = kv
    rows = metas[0].shape[1]
    width = xs[0].shape[1]
    slots = 4 * LATENTS
    batches = len(xs)
    scratch = pltpu.VMEM((rows, HEAD), F32)
    ys = [pltpu.VMEM((rows, width), BF16)] * (batches * (1 + routed))
    if riding:
        ys[-1] = pltpu.VMEM((rows + SPARE, width), BF16)
    switch = [] if flags is None else [flags]
    first = len(switch) + 2 + 2 * batches + len(squares) + len(before) + len(alts)
    return pl.pallas_call(
        functools.partial(
            layer_kernel,
            row,
            places,
            len(squares),
            len(before),
            riding,
            len(alts),
            routed,
            len(carry),
        ),
        out_shape=ys
        + [pltpu.VMEM((batches + len(before), rows), F32)]
        + [pltpu.VMEM(a.shape, a.dtype) for a in carry],
        in_specs=[IN_SMEM] * len(switch) + [IN_VMEM] * (first - len(switch) + len(carry)),
        out_specs=[IN_VMEM] * (len(ys) + 1 + len(carry)),
        scratch_shapes=[scratch] * 3 + [pltpu.VMEM((rows, HEAD), BF16)] + [scratch] * 2,
        input_output_aliases={first + i: len(ys) + 1 + i for i in range(len(carry))},
        compiler_params=pltpu.CompilerParams(vmem_limit_bytes=8 * MIB),
        cost_estimate=pl.CostEstimate(
            flops=FEW, bytes_accessed=0, transcendentals=0,
        ),
        name="layer",
    )(
        *switch,
        *[near(x) for x in xs],
        *metas,
        near(keys),
        near(vals),
        *[near(a) for a in (*squares, *before, *alts, *carry)],
    )


def place_kernel(lead, core, *refs):
    a, b, out, sems = refs[lead:]
    copies = [
        pltpu.make_async_copy(a, out.at[core[0]], sems.at[0]),
        pltpu.make_async_copy(b, out.at[core[0] ^ 1], sems.at[1]),
    ]
    for copy in copies:
        copy.start()
    for copy in copies:
        copy.wait()


def place(at, a, b, onto=None):
    lead = 0 if onto is None else 1
    return pl.pallas_call(
        functools.partial(place_kernel, lead),
        out_shape=jax.ShapeDtypeStruct((4, *a.shape), a.dtype),
        in_specs=[IN_SMEM] + [IN_HBM] * lead + [IN_VMEM] * 2,
        out_specs=IN_HBM,
        scratch_shapes=[pltpu.SemaphoreType.DMA((2,))],
        input_output_aliases={1: 0} if lead else {},
        compiler_params=pltpu.CompilerParams(vmem_limit_bytes=2 * MIB),
        name="place",
    )(at[None].astype(jnp.int32), *([] if onto is None else [onto]), near(a), near(b))


def body(
    features,
    latent_param,
    query_proj,
    key_proj,
    value_proj,
    out_proj,
    hidden,
    key_weight,
    value_weight,
    gate_angle,
    group_images,
    token_slot,
    attend,
):
    s = lax.axis_index("section")
    c = lax.axis_index("seq")
    m = lax.axis_index("mp")
    core = s & 1
    far = s >> 1
    mates = lax.axis_size("mp")
    seqs = lax.axis_size("seq")
    sections = lax.axis_size("section")

    def mp_swap(a, k):
        return lax.ppermute(a, "mp", [(i, i ^ k) for i in range(mates)])

    def core_swap(a):
        return lax.ppermute(a, "section", [(i, i ^ 1) for i in range(sections)])

    def far_swap(a):
        return lax.ppermute(a, "section", [(i, i ^ 2) for i in range(sections)])

    def cross(a):
        return lax.ppermute(a, "section", [(0, 2), (1, 3)])

    def spread(a):
        return [a] + [mp_swap(a, k) for k in (1, 2, 3)]

    other_w = (core_swap(key_weight), core_swap(value_weight))
    gate_own = jnp.broadcast_to(jnp.tanh(gate_angle)[:, None], (1, 128))
    gate_other = core_swap(gate_own)
    gate_first = jnp.where(core == 0, gate_own, gate_other)
    gate_second = jnp.where(core == 0, gate_other, gate_own)

    order = jnp.stack([m ^ 2, m ^ 1, m ^ 3, core, core + 2]).astype(jnp.int32)
    weights = (query_proj, key_proj, value_proj, out_proj)
    p2, p1, p3, squares = resample_sent(order, features, latent_param, hidden, weights)
    r2, r1, r3 = mp_swap(p2, 2), mp_swap(p1, 1), mp_swap(p3, 3)
    p0 = resample_own(m[None].astype(jnp.int32), features, latent_param, weights)
    latents, entering = combine(latent_param, squares, p0, (r1, r2, r3))

    inner = [(i, i ^ 1) for i in range(seqs)]
    outer = [(i, ((i + 1) ^ 1) - 1) for i in range(1, seqs - 1)]
    in_pair = lax.ppermute(latents, "seq", inner)
    across = lax.ppermute(latents, "seq", outer)
    odd = (c & 1) == 1
    firsts = group_images[:, 0, 0]
    start = lax.dynamic_index_in_dim(firsts, s, 0, keepdims=False)
    where_is = ((start + ((m - start) & 3)) >> 2) - c
    picked = jnp.where(
        where_is == 0, latents, jnp.where((where_is < 0) == odd, in_pair, across)
    )
    own_set = gather(spread(picked))
    far_set = far_swap(own_set)

    block = m ^ ((firsts[:, None] + token_slot[:, 0, :]) & 3)
    alive = attend[:, 0, :].astype(F32)
    rows = jnp.stack(
        [block.astype(F32), alive * gate_first, alive * gate_second]
        + [jnp.zeros_like(alive)] * 5,
        axis=1,
    )
    meta_own = lax.dynamic_index_in_dim(rows, s, 0, keepdims=False)
    meta_far = lax.dynamic_index_in_dim(rows, s ^ 2, 0, keepdims=False)

    own_w = (key_weight, value_weight)
    is_near = 1 - far

    flags = jnp.stack([core, is_near, core, core + 2]).astype(jnp.int32)
    flags_second = jnp.stack([1 - core, is_near]).astype(jnp.int32)
    k, v, tiles, hidden0, hidden1 = project(
        flags, [own_set], own_w, other_w, hidden, moved=2, keep=True
    )
    a0, qa0 = layer(1, [hidden0], [meta_own], (k, v), ((0, 0),), [entering])
    *second, tiles_second = project(flags_second, [own_set], own_w, other_w, hidden, keep=True)
    b0, _ = layer(2, [a0], [meta_own], second, ((0, 0),), spread(qa0), riding=True)
    x0 = cross(b0)
    kv = project_held(flags, far_set, tiles, [b0])
    a1, qa1 = layer(1, [hidden1], [meta_far], kv, ((0, 1),), [entering])
    kv = project_held(flags_second, far_set, tiles_second)
    b1, _ = layer(2, [a1], [meta_far], kv, ((0, 0),), spread(qa1), riding=True)
    x1 = cross(b1)

    flags = jnp.stack([core, far]).astype(jnp.int32)
    kv = project_both(flags, own_set, far_set, own_w, other_w)
    first, second = kv[:2], kv[2:]
    flags = jnp.stack([far, core]).astype(jnp.int32)
    c0, qc0, *second = layer(
        1, [x0], [meta_far], first, ((1, 0),), spread(from_line(x0, (b1, *first, *second))), carry=second
    )
    keep0, send0, _, *second = layer(
        2,
        [c0],
        [meta_far],
        second,
        ((1, 0),),
        spread(qc0),
        flags=flags,
        alts=(a0, b0),
        routed=True,
        carry=second,
    )
    c1, qc1 = layer(1, [x1], [meta_own], first, ((0, 0),), spread(from_line(x1, ())))
    keep1, send1, _ = layer(
        2, [c1], [meta_own], second, ((0, 0),), spread(qc1), flags=flags, alts=(a1, b1), routed=True
    )

    got0, got1 = core_swap(send0), core_swap(send1)
    out = place(core, keep0, got0)
    return place(core + 2, keep1, got1, out)[None]


def solution(mesh):
    return jax.shard_map(
        body,
        mesh=mesh,
        in_specs=(
            P(("section", "seq"), None, None),
            P(),
            P(None, "mp"),
            P(None, "mp"),
            P(None, "mp"),
            P("mp", None),
            P(None, "seq", "mp"),
            P("section", None, "mp"),
            P("section", None, "mp"),
            P("section"),
            P(None, "seq", None),
            P(None, "seq", None),
            P(None, "seq", None),
        ),
        out_specs=P("section", None, "seq", "mp"),
        check_vma=False,
    )
```

```python
import functools

import jax
import jax.numpy as jnp
from jax import lax
from jax.experimental import pallas as pl
from jax.experimental.pallas import tpu as pltpu
from jax.sharding import PartitionSpec as P

D = 8192
HEAD = 128
LATENTS = 64
PHEAD = 96
EPS = 1e-05
NEG = -1e30
LOG2E = 1.4426950408889634
F32 = jnp.float32
BF16 = jnp.bfloat16
MIB = 1024 * 1024
FEW = 1000
SPARE = 16


def normalize(v):
    mean = jnp.mean(v, axis=-1, keepdims=True)
    cent = v - mean
    var = jnp.mean(cent * cent, axis=-1, keepdims=True)
    return cent * lax.rsqrt(var + EPS)


def dot(a, b):
    return jnp.dot(a, b, preferred_element_type=F32)


def dot_nt(a, b):
    return lax.dot_general(a, b, (((1,), (1,)), ((), ())), preferred_element_type=F32)


def up16(n):
    return -(-n // 16) * 16


def up128(n):
    return -(-n // 128) * 128


def near(a):
    return pltpu.with_memory_space_constraint(a, pltpu.VMEM)


def away(a):
    return pltpu.with_memory_space_constraint(a, pltpu.HBM)


IN_VMEM = pl.BlockSpec(memory_space=pltpu.VMEM)
IN_SMEM = pl.BlockSpec(memory_space=pltpu.SMEM)
IN_HBM = pl.BlockSpec(memory_space=pltpu.HBM)


def resample_updates(frames, lat, weights, held, ctx, tail, pk, pv, pqm, mixed, sems):
    n = len(frames)
    patches = frames[0].shape[0]
    keys = LATENTS + patches
    rows = up16(keys)
    qp, kp, vp, op = held
    inner = qp.shape[1]
    heads = inner // PHEAD
    cut = inner // 256 * 256
    side = inner - cut
    loads = [pltpu.make_async_copy(a, b, sems.at[i]) for i, (a, b) in enumerate(zip(weights, held))]
    for i in (1, 2, 0, 3):
        loads[i].start()

    base = normalize(lat[...].astype(F32)).astype(BF16)
    for i in range(n):
        top = i * rows
        ctx[top : top + LATENTS, :] = base
        ctx[top + rows - 16 : top + rows, :] = jnp.zeros((16, ctx.shape[1]), BF16)
        for r in range(0, patches, 64):
            end = min(r + 64, patches)
            block = normalize(frames[i][r:end, :].astype(F32)).astype(BF16)
            ctx[top + LATENTS + r : top + LATENTS + end, :] = block
    pv[:, inner:] = jnp.ones((pv.shape[0], 128), BF16)

    for i in (1, 2):
        loads[i].wait()
    tail[:, :side] = kp[:, cut:]
    tail[:, side:] = vp[:, cut:]
    pk[:, :cut] = dot(ctx[...], kp[:, :cut]).astype(BF16)
    pv[:, :cut] = dot(ctx[...], vp[:, :cut]).astype(BF16)
    both = dot(ctx[...], tail[...]).astype(BF16)
    pk[:, cut:] = both[:, :side]
    pv[:, cut:inner] = both[:, side:]
    loads[0].wait()
    pq = dot(base, qp[...]).astype(BF16).astype(F32)
    which = lax.broadcasted_iota(jnp.int32, (LATENTS, inner), 1) // PHEAD
    for h in range(heads):
        pqm[h * LATENTS : (h + 1) * LATENTS, :] = jnp.where(which == h, pq, 0.0).astype(BF16)

    for i in range(n):
        own = slice(i * rows, (i + 1) * rows)
        score = dot_nt(pqm[...], pk[own, :]) * (PHEAD ** (-0.5) * LOG2E)
        lane = lax.broadcasted_iota(jnp.int32, score.shape, 1)
        score = jnp.where(lane < keys, score, NEG)
        e = jnp.exp2(score - jnp.max(score, axis=1, keepdims=True)).astype(BF16)
        mix = dot(e, pv[own, :])
        inverse = 1.0 / mix[:, inner:]
        for j in range(inner // 128):
            at = lax.broadcasted_iota(jnp.int32, (LATENTS, 128), 1) + j * 128
            tile = jnp.zeros((LATENTS, 128), F32)
            for h in range(j * 128 // PHEAD, (j * 128 + 127) // PHEAD + 1):
                rows_h = slice(h * LATENTS, (h + 1) * LATENTS)
                value = mix[rows_h, j * 128 : (j + 1) * 128] * inverse[rows_h, :]
                tile = jnp.where(at // PHEAD == h, value, tile)
            mixed[i * LATENTS : (i + 1) * LATENTS, j * 128 : (j + 1) * 128] = tile.astype(BF16)
    loads[3].wait()
    return dot(mixed[...], op[...])


def resample_scratch(n, patches, vdim, inner, weights):
    rows = n * up16(LATENTS + patches)
    cut = inner // 256 * 256
    return [pltpu.VMEM(w.shape, BF16) for w in weights] + [
        pltpu.VMEM((rows, vdim), BF16),
        pltpu.VMEM((vdim, 2 * (inner - cut)), BF16),
        pltpu.VMEM((rows, inner), BF16),
        pltpu.VMEM((rows, inner + 128), BF16),
        pltpu.VMEM((inner // PHEAD * LATENTS, inner), BF16),
        pltpu.VMEM((n * LATENTS, inner), BF16),
        pltpu.SemaphoreType.DMA((4,)),
    ]


def resample_sent_kernel(n, ids, lat, feat, hid, *refs):
    weights, sent, squares, refs = refs[:4], refs[4 : 4 + n], refs[4 + n], refs[5 + n :]
    near_hid, hid_sems = refs[0:2], refs[2]
    loads = [
        pltpu.make_async_copy(hid.at[ids[n + i]], near_hid[i], hid_sems.at[i]) for i in range(2)
    ]
    frames = [feat.at[ids[i]] for i in range(n)]
    update = resample_updates(frames, lat, weights, refs[3:7], *refs[7:])
    for load in loads:
        load.start()
    for i in range(n):
        sent[i][0:LATENTS, :] = update[i * LATENTS : (i + 1) * LATENTS].astype(BF16)
    lines = []
    for load, a in zip(loads, near_hid):
        load.wait()
        acc = jnp.zeros((a.shape[0], 128), F32)
        for at in range(0, a.shape[1], 128):
            v = a[:, at : at + 128].astype(F32)
            acc = acc + v * v
        lines.append(jnp.sum(acc.T, axis=0, keepdims=True))
    squares[...] = jnp.concatenate(lines, axis=0)
    line = as_line(lines, sent[0].shape[1])
    for i in range(n):
        sent[i][LATENTS:, :] = line


def resample_sent(ids, features, latent_param, hidden, weights):
    n = ids.shape[0] - 2
    _, patches, vdim = features.shape
    _, rows, width = hidden.shape
    inner = weights[0].shape[1]
    return pl.pallas_call(
        functools.partial(resample_sent_kernel, n),
        out_shape=[pltpu.VMEM((LATENTS + SPARE, vdim), BF16)] * n
        + [pltpu.VMEM((2, rows), F32)],
        in_specs=[IN_SMEM, IN_VMEM, IN_VMEM] + [IN_HBM] * 5,
        out_specs=[IN_VMEM] * (n + 1),
        scratch_shapes=[pltpu.VMEM((rows, width), BF16)] * 2
        + [pltpu.SemaphoreType.DMA((2,))]
        + resample_scratch(n, patches, vdim, inner, weights),
        compiler_params=pltpu.CompilerParams(vmem_limit_bytes=24 * MIB),
        name="resample",
    )(ids, latent_param, near(features), away(hidden), *[away(w) for w in weights])


def resample_own_kernel(ids, lat, feat, *refs):
    refs[4][...] = resample_updates([feat.at[ids[0]]], lat, refs[:4], refs[5:9], *refs[9:])


def resample_own(ids, features, latent_param, weights):
    _, patches, vdim = features.shape
    inner = weights[0].shape[1]
    return pl.pallas_call(
        resample_own_kernel,
        out_shape=pltpu.VMEM((LATENTS, vdim), F32),
        in_specs=[IN_SMEM, IN_VMEM, IN_VMEM] + [IN_HBM] * 4,
        out_specs=IN_VMEM,
        scratch_shapes=resample_scratch(1, patches, vdim, inner, weights),
        compiler_params=pltpu.CompilerParams(vmem_limit_bytes=16 * MIB),
        name="resample",
    )(ids, latent_param, near(features), *[away(w) for w in weights])


def combine_kernel(lat, squares, own, a, b, c, out, total_squares):
    total = own[...]
    sums = squares[...]
    count = squares.shape[0]
    for part in (a, b, c):
        total = total + part[:LATENTS, :].astype(F32)
        line = part[LATENTS:, :].astype(F32)[0:1, :]
        at = lambda i: line[:, i * 128 : (i + 1) * 128]
        sums = sums + jnp.concatenate([at(i) + at(count + i) for i in range(count)], axis=0)
    out[...] = normalize(lat[...].astype(F32) + total).astype(BF16)
    total_squares[...] = sums


def combine(latent_param, squares, own, parts):
    return pl.pallas_call(
        combine_kernel,
        out_shape=[
            pltpu.VMEM(latent_param.shape, BF16),
            pltpu.VMEM(squares.shape, F32),
        ],
        in_specs=[IN_VMEM] * 6,
        out_specs=[IN_VMEM] * 2,
        compiler_params=pltpu.CompilerParams(vmem_limit_bytes=8 * MIB),
        name="combine",
    )(latent_param, squares, near(own), *[near(p) for p in parts])


TILE = 1024
AHEAD = 2


def project_kernel(count, moved, flags, *refs):
    chunks, refs = refs[:count], refs[count:]
    hid, own_k, own_v, other_k, other_v = refs[:5]
    keys, vals, tiles = refs[5:8]
    near_hid = refs[8 : 8 + moved]
    chosen, sems, hid_sems = refs[8 + moved :]
    steps = 2 * (keys.shape[1] // TILE)

    def fetch(step, src):
        cols = pl.ds(pl.multiple_of(step // 2 * TILE, TILE), TILE)
        return pltpu.make_async_copy(src.at[0, :, cols], tiles.at[step], sems.at[step])

    def start(step, odd):
        of_own, of_other = (own_v, other_v) if odd else (own_k, other_k)

        @pl.when(flags[0] == 0)
        def _():
            fetch(step, of_own).start()

        @pl.when(flags[0] != 0)
        def _():
            fetch(step, of_other).start()

    @pl.when(flags[1] != 0)
    def _():
        for step in range(AHEAD):
            start(step, step % 2)
        loads = [
            pltpu.make_async_copy(hid.at[flags[2 + i]], near_hid[i], hid_sems.at[i])
            for i in range(moved)
        ]
        for load in loads:
            load.start()
        top = 0
        for a in chunks:
            chosen[top : top + a.shape[0], :] = a[...]
            top += a.shape[0]

        def column(j, carry):
            cols = pl.ds(pl.multiple_of(j * TILE, TILE), TILE)
            for i, out in enumerate((keys, vals)):
                step = 2 * j + i
                fetch(step, own_k).wait()

                @pl.when(step + AHEAD < steps)
                def _():
                    start(step + AHEAD, (i + AHEAD) % 2)

                out[:, cols] = dot(chosen[...], tiles[step]).astype(BF16)
            return carry

        lax.fori_loop(0, steps // 2, column, 0)
        for load in loads:
            load.wait()


def project(flags, chunks, own, other, hidden, moved=0, keep=False):
    vdim, width = own[0].shape[1:]
    rows = sum(a.shape[0] for a in chunks)
    steps = 2 * (width // TILE)
    held = pltpu.VMEM((steps, vdim, TILE), BF16)
    kernel = functools.partial(project_kernel, len(chunks), moved)
    if not keep:
        inner = kernel

        def kernel(*refs):
            at = 1 + len(chunks) + 7
            refs, tiles = refs[:-1], refs[-1]
            return inner(*refs[:at], tiles, *refs[at:])

    return pl.pallas_call(
        kernel,
        out_shape=[pltpu.VMEM((rows, width), BF16)] * 2
        + [held] * keep
        + [pltpu.VMEM(hidden.shape[1:], BF16)] * moved,
        in_specs=[IN_SMEM] + [IN_VMEM] * len(chunks) + [IN_HBM] * 5,
        out_specs=[IN_VMEM] * (2 + keep + moved),
        scratch_shapes=[
            pltpu.VMEM((rows, vdim), BF16),
            pltpu.SemaphoreType.DMA((steps,)),
            pltpu.SemaphoreType.DMA((2,)),
        ]
        + [held] * (not keep),
        compiler_params=pltpu.CompilerParams(vmem_limit_bytes=(8 if keep else 20) * MIB),
        cost_estimate=pl.CostEstimate(
            flops=FEW, bytes_accessed=0, transcendentals=0
        ),
        name="project",
    )(flags, *[near(a) for a in chunks], *[away(a) for a in (hidden, *own, *other)])


def project_both_kernel(flags, a, b, own_k, own_v, other_k, other_v, k1, v1, k2, v2, chosen, ring, sems):
    part = a.shape[0]
    half = 2 * (k1.shape[1] // TILE)
    depth = ring.shape[0]

    def fetch(step, src):
        cols = pl.ds(pl.multiple_of(step % half // 2 * TILE, TILE), TILE)
        return pltpu.make_async_copy(src.at[0, :, cols], ring.at[step % depth], sems.at[step % depth])

    def start(step, odd):
        of_own, of_other = (own_v, other_v) if odd else (own_k, other_k)
        from_own = (step // half) == flags[0]

        @pl.when(from_own)
        def _():
            fetch(step, of_own).start()

        @pl.when(jnp.logical_not(from_own))
        def _():
            fetch(step, of_other).start()

    @pl.when(flags[1] != 0)
    def _():
        for step in range(depth - 1):
            start(step, step % 2)
        chosen[0:part, :] = a[...]
        chosen[part:, :] = b[...]
        for which, outs in enumerate(((k1, v1), (k2, v2))):

            def column(j, carry, which=which, outs=outs):
                cols = pl.ds(pl.multiple_of(j * TILE, TILE), TILE)
                for i, out in enumerate(outs):
                    step = which * half + 2 * j + i
                    fetch(step, own_k).wait()

                    @pl.when(step + depth - 1 < 2 * half)
                    def _():
                        start(step + depth - 1, (i + depth - 1) % 2)

                    out[:, cols] = dot(chosen[...], ring[step % depth]).astype(BF16)
                return carry

            lax.fori_loop(0, half // 2, column, 0)


def project_both(flags, a, b, own, other):
    vdim, width = own[0].shape[1:]
    rows = a.shape[0] + b.shape[0]
    return pl.pallas_call(
        project_both_kernel,
        out_shape=[pltpu.VMEM((rows, width), BF16)] * 4,
        in_specs=[IN_SMEM, IN_VMEM, IN_VMEM] + [IN_HBM] * 4,
        out_specs=[IN_VMEM] * 4,
        scratch_shapes=[
            pltpu.VMEM((rows, vdim), BF16),
            pltpu.VMEM((AHEAD + 1, vdim, TILE), BF16),
            pltpu.SemaphoreType.DMA((AHEAD + 1,)),
        ],
        compiler_params=pltpu.CompilerParams(vmem_limit_bytes=16 * MIB),
        cost_estimate=pl.CostEstimate(flops=FEW, bytes_accessed=0, transcendentals=0),
        name="project",
    )(flags, near(a), near(b), *[away(w) for w in (*own, *other)])


def project_held_kernel(flags, a, tiles, *refs):
    keys, vals = refs[-2:]

    @pl.when(flags[1] != 0)
    def _():
        def column(j, carry):
            cols = pl.ds(pl.multiple_of(j * TILE, TILE), TILE)
            keys[:, cols] = dot(a[...], tiles[2 * j]).astype(BF16)
            vals[:, cols] = dot(a[...], tiles[2 * j + 1]).astype(BF16)
            return carry

        lax.fori_loop(0, keys.shape[1] // TILE, column, 0)


def project_held(flags, a, tiles, after=()):
    steps, vdim, _ = tiles.shape
    rows = a.shape[0]
    width = steps // 2 * TILE
    return pl.pallas_call(
        project_held_kernel,
        out_shape=[pltpu.VMEM((rows, width), BF16)] * 2,
        in_specs=[IN_SMEM] + [IN_VMEM] * (2 + len(after)),
        out_specs=[IN_VMEM] * 2,
        compiler_params=pltpu.CompilerParams(vmem_limit_bytes=8 * MIB),
        cost_estimate=pl.CostEstimate(
            flops=FEW, bytes_accessed=0, transcendentals=0
        ),
        name="project",
    )(flags, near(a), near(tiles), *[near(b) for b in after])


def gather_kernel(*refs):
    for i, a in enumerate(refs[:-1]):
        refs[-1][i * LATENTS : (i + 1) * LATENTS, :] = a[...]


def gather(chunks):
    vdim = chunks[0].shape[1]
    return pl.pallas_call(
        gather_kernel,
        out_shape=pltpu.VMEM((len(chunks) * LATENTS, vdim), BF16),
        in_specs=[IN_VMEM] * len(chunks),
        out_specs=IN_VMEM,
        compiler_params=pltpu.CompilerParams(vmem_limit_bytes=2 * MIB),
        name="gather",
    )(*[near(a) for a in chunks])


def as_line(lines, width):
    high = [line.astype(BF16).astype(F32) for line in lines]
    low = [line - h for line, h in zip(lines, high)]
    parts = high + low
    spare = jnp.zeros((1, width - len(parts) * parts[0].shape[1]), F32)
    line = jnp.concatenate(parts + [spare], axis=1)
    first = lax.broadcasted_iota(jnp.int32, (SPARE, width), 0) == 0
    return jnp.where(first, line, 0.0).astype(BF16)


def from_line_kernel(x, *refs):
    out = refs[-1]
    line = x[x.shape[0] - SPARE :, :].astype(F32)[0:1, :]
    at = lambda i: line[:, i * 128 : (i + 1) * 128]
    count = out.shape[0]
    out[...] = jnp.concatenate([at(i) + at(count + i) for i in range(count)], axis=0)


def from_line(x, after):
    return pl.pallas_call(
        from_line_kernel,
        out_shape=pltpu.VMEM((1, 128), F32),
        in_specs=[IN_VMEM] * (1 + len(after)),
        out_specs=IN_VMEM,
        compiler_params=pltpu.CompilerParams(vmem_limit_bytes=2 * MIB),
        name="from_line",
    )(near(x), *[near(a) for a in after])


def layer_kernel(row, places, count, ahead, riding, others, routed, carried, *refs):
    batches = len(places)
    flags, refs = (refs[0], refs[1:]) if others else (None, refs)
    xs, metas, refs = refs[:batches], refs[batches : 2 * batches], refs[2 * batches :]
    keys, vals, refs = refs[0], refs[1], refs[2:]
    squares, before, refs = refs[:count], refs[count : count + ahead], refs[count + ahead :]
    alts, refs = refs[:others], refs[others + carried :]
    outs, refs = refs[: batches * (1 + routed)], refs[batches * (1 + routed) :]
    square_out, refs = refs[0], refs[1 + carried :]
    scale_s, bias_s, high_s, half_s, gate_s, acc = refs
    rows = metas[0].shape[1]
    heads = xs[0].shape[1] // HEAD
    slots = 4 * LATENTS

    def write(i, cols, old, new):
        if routed:
            outs[2 * i][:, cols] = jnp.where(flags[1] == 0, old, new)
            outs[2 * i + 1][:, cols] = jnp.where(flags[1] == 0, new, old)
        else:
            outs[i][0:rows, cols] = new

    def run():
        total = squares[0][...]
        for part in squares[1:]:
            total = total + part[...]
        ones = jnp.ones((slots, HEAD), BF16)
        lines = [b[...] for b in before]
        for i, (at, line) in enumerate(places):
            scale = lax.rsqrt(total[line : line + 1, :] / D + EPS) * (HEAD ** (-0.5) * LOG2E)
            spare = jnp.zeros((rows - 3, rows), F32)
            gate = metas[i][row : row + 1, :]
            cols = jnp.concatenate([scale, metas[i][0:1, :], gate, spare], axis=0).T
            slot = jnp.broadcast_to(cols[:, 1:2], (rows, HEAD))
            scale_s[...] = jnp.broadcast_to(cols[:, 0:1], (rows, HEAD))
            gate_s[...] = jnp.broadcast_to(cols[:, 2:3], (rows, HEAD))
            upper = jnp.where(slot > 1.5, 1.0, 0.0)
            high_s[...] = upper
            half_s[...] = upper.astype(BF16)
            half = (lax.broadcasted_iota(jnp.int32, (rows, HEAD), 1) // LATENTS).astype(F32)
            bias_s[...] = jnp.where(slot - 2.0 * upper == half, 0.0, NEG)
            high = high_s[...] > 0.5
            sums = jnp.zeros((rows, HEAD), F32)
            for h in range(heads):
                cols = slice(h * HEAD, (h + 1) * HEAD)
                k = keys[at * slots : (at + 1) * slots, cols]
                v = vals[at * slots : (at + 1) * slots, cols]
                q = xs[i][0:rows, cols]
                score = dot_nt(q, k)
                t = jnp.where(high, score[:, HEAD:], score[:, :HEAD]) * scale_s[...] + bias_s[...]
                e = jnp.exp2(t - jnp.max(t, axis=1, keepdims=True)).astype(BF16)
                e_high = e * half_s[...]
                weight = jnp.concatenate([e - e_high, e_high], axis=1)
                mixed = dot(weight, jnp.concatenate([v, ones], axis=1))
                attn = mixed[:, :HEAD] / mixed[:, HEAD:]
                out = (q.astype(F32) + gate_s[...] * attn).astype(BF16)
                write(i, cols, q, out)
                of = out.astype(F32)
                sums = sums + of * of
            acc[...] = sums
            lines.append(jnp.sum(acc[...].T, axis=0, keepdims=True))
        square_out[...] = jnp.concatenate(lines, axis=0)
        if riding:
            outs[-1][rows:, :] = as_line(lines, outs[-1].shape[1])

    if not others:
        run()
        return
    pl.when(flags[0] != 0)(run)

    @pl.when(flags[0] == 0)
    def _():
        for i in range(batches):
            for h in range(heads):
                cols = slice(h * HEAD, (h + 1) * HEAD)
                write(i, cols, alts[i][0:rows, cols], alts[batches + i][0:rows, cols])
        square_out[...] = jnp.zeros_like(square_out)


def layer(
    row, xs, metas, kv, places, squares, before=(), riding=False, flags=None, alts=(), routed=False, carry=()
):
    keys, vals = kv
    rows = metas[0].shape[1]
    width = xs[0].shape[1]
    slots = 4 * LATENTS
    batches = len(xs)
    scratch = pltpu.VMEM((rows, HEAD), F32)
    ys = [pltpu.VMEM((rows, width), BF16)] * (batches * (1 + routed))
    if riding:
        ys[-1] = pltpu.VMEM((rows + SPARE, width), BF16)
    switch = [] if flags is None else [flags]
    first = len(switch) + 2 + 2 * batches + len(squares) + len(before) + len(alts)
    return pl.pallas_call(
        functools.partial(
            layer_kernel,
            row,
            places,
            len(squares),
            len(before),
            riding,
            len(alts),
            routed,
            len(carry),
        ),
        out_shape=ys
        + [pltpu.VMEM((batches + len(before), rows), F32)]
        + [pltpu.VMEM(a.shape, a.dtype) for a in carry],
        in_specs=[IN_SMEM] * len(switch) + [IN_VMEM] * (first - len(switch) + len(carry)),
        out_specs=[IN_VMEM] * (len(ys) + 1 + len(carry)),
        scratch_shapes=[scratch] * 3 + [pltpu.VMEM((rows, HEAD), BF16)] + [scratch] * 2,
        input_output_aliases={first + i: len(ys) + 1 + i for i in range(len(carry))},
        compiler_params=pltpu.CompilerParams(vmem_limit_bytes=8 * MIB),
        cost_estimate=pl.CostEstimate(
            flops=FEW, bytes_accessed=0, transcendentals=0,
        ),
        name="layer",
    )(
        *switch,
        *[near(x) for x in xs],
        *metas,
        near(keys),
        near(vals),
        *[near(a) for a in (*squares, *before, *alts, *carry)],
    )


def place_kernel(lead, core, *refs):
    a, b, out, sems = refs[lead:]
    copies = [
        pltpu.make_async_copy(a, out.at[core[0]], sems.at[0]),
        pltpu.make_async_copy(b, out.at[core[0] ^ 1], sems.at[1]),
    ]
    for copy in copies:
        copy.start()
    for copy in copies:
        copy.wait()


def place(at, a, b, onto=None):
    lead = 0 if onto is None else 1
    return pl.pallas_call(
        functools.partial(place_kernel, lead),
        out_shape=jax.ShapeDtypeStruct((4, *a.shape), a.dtype),
        in_specs=[IN_SMEM] + [IN_HBM] * lead + [IN_VMEM] * 2,
        out_specs=IN_HBM,
        scratch_shapes=[pltpu.SemaphoreType.DMA((2,))],
        input_output_aliases={1: 0} if lead else {},
        compiler_params=pltpu.CompilerParams(vmem_limit_bytes=2 * MIB),
        name="place",
    )(at[None].astype(jnp.int32), *([] if onto is None else [onto]), near(a), near(b))


def body(
    features,
    latent_param,
    query_proj,
    key_proj,
    value_proj,
    out_proj,
    hidden,
    key_weight,
    value_weight,
    gate_angle,
    group_images,
    token_slot,
    attend,
):
    s = lax.axis_index("section")
    c = lax.axis_index("seq")
    m = lax.axis_index("mp")
    core = s & 1
    far = s >> 1
    mates = lax.axis_size("mp")
    seqs = lax.axis_size("seq")
    sections = lax.axis_size("section")

    def mp_swap(a, k):
        return lax.ppermute(a, "mp", [(i, i ^ k) for i in range(mates)])

    def core_swap(a):
        return lax.ppermute(a, "section", [(i, i ^ 1) for i in range(sections)])

    def far_swap(a):
        return lax.ppermute(a, "section", [(i, i ^ 2) for i in range(sections)])

    def cross(a):
        return lax.ppermute(a, "section", [(0, 2), (1, 3)])

    def spread(a):
        return [a] + [mp_swap(a, k) for k in (1, 2, 3)]

    other_w = (core_swap(key_weight), core_swap(value_weight))
    gate_own = jnp.broadcast_to(jnp.tanh(gate_angle)[:, None], (1, 128))
    gate_other = core_swap(gate_own)
    gate_first = jnp.where(core == 0, gate_own, gate_other)
    gate_second = jnp.where(core == 0, gate_other, gate_own)

    order = jnp.stack([m ^ 2, m ^ 1, m ^ 3, core, core + 2]).astype(jnp.int32)
    weights = (query_proj, key_proj, value_proj, out_proj)
    p2, p1, p3, squares = resample_sent(order, features, latent_param, hidden, weights)
    r2, r1, r3 = mp_swap(p2, 2), mp_swap(p1, 1), mp_swap(p3, 3)
    p0 = resample_own(m[None].astype(jnp.int32), features, latent_param, weights)
    latents, entering = combine(latent_param, squares, p0, (r1, r2, r3))

    inner = [(i, i ^ 1) for i in range(seqs)]
    outer = [(i, (((i + 1) ^ 1) - 1) % seqs) for i in range(seqs)]
    in_pair = lax.ppermute(latents, "seq", inner)
    across = lax.ppermute(latents, "seq", outer)
    odd = (c & 1) == 1
    firsts = group_images[:, 0, 0]
    start = lax.dynamic_index_in_dim(firsts, s, 0, keepdims=False)
    where_is = ((start + ((m - start) & 3)) >> 2) - c
    picked = jnp.where(
        where_is == 0, latents, jnp.where((where_is < 0) == odd, in_pair, across)
    )
    own_set = gather(spread(picked))
    far_set = far_swap(own_set)

    block = m ^ ((firsts[:, None] + token_slot[:, 0, :]) & 3)
    alive = attend[:, 0, :].astype(F32)
    rows = jnp.stack(
        [block.astype(F32), alive * gate_first, alive * gate_second]
        + [jnp.zeros_like(alive)] * 5,
        axis=1,
    )
    meta_own = lax.dynamic_index_in_dim(rows, s, 0, keepdims=False)
    meta_far = lax.dynamic_index_in_dim(rows, s ^ 2, 0, keepdims=False)

    own_w = (key_weight, value_weight)
    is_near = 1 - far

    flags = jnp.stack([core, is_near, core, core + 2]).astype(jnp.int32)
    flags_second = jnp.stack([1 - core, is_near]).astype(jnp.int32)
    k, v, tiles, hidden0, hidden1 = project(
        flags, [own_set], own_w, other_w, hidden, moved=2, keep=True
    )
    a0, qa0 = layer(1, [hidden0], [meta_own], (k, v), ((0, 0),), [entering])
    *second, tiles_second = project(flags_second, [own_set], own_w, other_w, hidden, keep=True)
    b0, _ = layer(2, [a0], [meta_own], second, ((0, 0),), spread(qa0), riding=True)
    x0 = cross(b0)
    kv = project_held(flags, far_set, tiles, [b0])
    a1, qa1 = layer(1, [hidden1], [meta_far], kv, ((0, 1),), [entering])
    kv = project_held(flags_second, far_set, tiles_second)
    b1, _ = layer(2, [a1], [meta_far], kv, ((0, 0),), spread(qa1), riding=True)
    x1 = cross(b1)

    flags = jnp.stack([core, far]).astype(jnp.int32)
    kv = project_both(flags, own_set, far_set, own_w, other_w)
    first, second = kv[:2], kv[2:]
    flags = jnp.stack([far, core]).astype(jnp.int32)
    c0, qc0, *second = layer(
        1, [x0], [meta_far], first, ((1, 0),), spread(from_line(x0, (b1, *first, *second))), carry=second
    )
    keep0, send0, _, *second = layer(
        2,
        [c0],
        [meta_far],
        second,
        ((1, 0),),
        spread(qc0),
        flags=flags,
        alts=(a0, b0),
        routed=True,
        carry=second,
    )
    c1, qc1 = layer(1, [x1], [meta_own], first, ((0, 0),), spread(from_line(x1, ())))
    keep1, send1, _ = layer(
        2, [c1], [meta_own], second, ((0, 0),), spread(qc1), flags=flags, alts=(a1, b1), routed=True
    )

    got0, got1 = core_swap(send0), core_swap(send1)
    out = place(core, keep0, got0)
    return place(core + 2, keep1, got1, out)[None]


def solution(mesh):
    return jax.shard_map(
        body,
        mesh=mesh,
        in_specs=(
            P(("section", "seq"), None, None),
            P(),
            P(None, "mp"),
            P(None, "mp"),
            P(None, "mp"),
            P("mp", None),
            P(None, "seq", "mp"),
            P("section", None, "mp"),
            P("section", None, "mp"),
            P("section"),
            P(None, "seq", None),
            P(None, "seq", None),
            P(None, "seq", None),
        ),
        out_specs=P("section", None, "seq", "mp"),
        check_vma=False,
    )
```

```python
import functools

import jax
import jax.numpy as jnp
from jax import lax
from jax.experimental import pallas as pl
from jax.experimental.pallas import tpu as pltpu
from jax.sharding import PartitionSpec as P

D = 8192
HEAD = 128
LATENTS = 64
PHEAD = 96
EPS = 1e-05
NEG = -1e30
LOG2E = 1.4426950408889634
F32 = jnp.float32
BF16 = jnp.bfloat16
MIB = 1024 * 1024
FEW = 1000
SPARE = 16


def normalize(v):
    mean = jnp.mean(v, axis=-1, keepdims=True)
    cent = v - mean
    var = jnp.mean(cent * cent, axis=-1, keepdims=True)
    return cent * lax.rsqrt(var + EPS)


def dot(a, b):
    return jnp.dot(a, b, preferred_element_type=F32)


def dot_nt(a, b):
    return lax.dot_general(a, b, (((1,), (1,)), ((), ())), preferred_element_type=F32)


def up16(n):
    return -(-n // 16) * 16


def up128(n):
    return -(-n // 128) * 128


def near(a):
    return pltpu.with_memory_space_constraint(a, pltpu.VMEM)


def away(a):
    return pltpu.with_memory_space_constraint(a, pltpu.HBM)


IN_VMEM = pl.BlockSpec(memory_space=pltpu.VMEM)
IN_SMEM = pl.BlockSpec(memory_space=pltpu.SMEM)
IN_HBM = pl.BlockSpec(memory_space=pltpu.HBM)


def resample_updates(frames, lat, weights, held, ctx, tail, pk, pv, pqm, mixed, sems, midway=()):
    n = len(frames)
    patches = frames[0].shape[0]
    keys = LATENTS + patches
    rows = up16(keys)
    qp, kp, vp, op = held
    inner = qp.shape[1]
    heads = inner // PHEAD
    cut = inner // 256 * 256
    side = inner - cut
    loads = [pltpu.make_async_copy(a, b, sems.at[i]) for i, (a, b) in enumerate(zip(weights, held))]
    for i in (1, 2, 0, 3):
        loads[i].start()

    base = normalize(lat[...].astype(F32)).astype(BF16)
    for i in range(n):
        top = i * rows
        ctx[top : top + LATENTS, :] = base
        ctx[top + rows - 16 : top + rows, :] = jnp.zeros((16, ctx.shape[1]), BF16)
        for r in range(0, patches, 64):
            end = min(r + 64, patches)
            block = normalize(frames[i][r:end, :].astype(F32)).astype(BF16)
            ctx[top + LATENTS + r : top + LATENTS + end, :] = block
    pv[:, inner:] = jnp.ones((pv.shape[0], 128), BF16)

    for i in (1, 2):
        loads[i].wait()
    tail[:, :side] = kp[:, cut:]
    tail[:, side:] = vp[:, cut:]
    pk[:, :cut] = dot(ctx[...], kp[:, :cut]).astype(BF16)
    pv[:, :cut] = dot(ctx[...], vp[:, :cut]).astype(BF16)
    both = dot(ctx[...], tail[...]).astype(BF16)
    pk[:, cut:] = both[:, :side]
    pv[:, cut:inner] = both[:, side:]
    loads[0].wait()
    for load in midway:
        load.start()
    pq = dot(base, qp[...]).astype(BF16).astype(F32)
    which = lax.broadcasted_iota(jnp.int32, (LATENTS, inner), 1) // PHEAD
    for h in range(heads):
        pqm[h * LATENTS : (h + 1) * LATENTS, :] = jnp.where(which == h, pq, 0.0).astype(BF16)

    for i in range(n):
        own = slice(i * rows, (i + 1) * rows)
        score = dot_nt(pqm[...], pk[own, :]) * (PHEAD ** (-0.5) * LOG2E)
        lane = lax.broadcasted_iota(jnp.int32, score.shape, 1)
        score = jnp.where(lane < keys, score, NEG)
        e = jnp.exp2(score - jnp.max(score, axis=1, keepdims=True)).astype(BF16)
        mix = dot(e, pv[own, :])
        inverse = 1.0 / mix[:, inner:]
        for j in range(inner // 128):
            at = lax.broadcasted_iota(jnp.int32, (LATENTS, 128), 1) + j * 128
            tile = jnp.zeros((LATENTS, 128), F32)
            for h in range(j * 128 // PHEAD, (j * 128 + 127) // PHEAD + 1):
                rows_h = slice(h * LATENTS, (h + 1) * LATENTS)
                value = mix[rows_h, j * 128 : (j + 1) * 128] * inverse[rows_h, :]
                tile = jnp.where(at // PHEAD == h, value, tile)
            mixed[i * LATENTS : (i + 1) * LATENTS, j * 128 : (j + 1) * 128] = tile.astype(BF16)
    loads[3].wait()
    return dot(mixed[...], op[...])


def resample_scratch(n, patches, vdim, inner, weights):
    rows = n * up16(LATENTS + patches)
    cut = inner // 256 * 256
    return [pltpu.VMEM(w.shape, BF16) for w in weights] + [
        pltpu.VMEM((rows, vdim), BF16),
        pltpu.VMEM((vdim, 2 * (inner - cut)), BF16),
        pltpu.VMEM((rows, inner), BF16),
        pltpu.VMEM((rows, inner + 128), BF16),
        pltpu.VMEM((inner // PHEAD * LATENTS, inner), BF16),
        pltpu.VMEM((n * LATENTS, inner), BF16),
        pltpu.SemaphoreType.DMA((4,)),
    ]


def resample_sent_kernel(n, ids, lat, feat, hid, *refs):
    weights, sent, squares, refs = refs[:4], refs[4 : 4 + n], refs[4 + n], refs[5 + n :]
    near_hid, hid_sems = refs[0:2], refs[2]
    loads = [
        pltpu.make_async_copy(hid.at[ids[n + i]], near_hid[i], hid_sems.at[i]) for i in range(2)
    ]
    frames = [feat.at[ids[i]] for i in range(n)]
    update = resample_updates(frames, lat, weights, refs[3:7], *refs[7:], midway=loads)
    for i in range(n):
        sent[i][0:LATENTS, :] = update[i * LATENTS : (i + 1) * LATENTS].astype(BF16)
    lines = []
    for load, a in zip(loads, near_hid):
        load.wait()
        acc = jnp.zeros((a.shape[0], 128), F32)
        for at in range(0, a.shape[1], 128):
            v = a[:, at : at + 128].astype(F32)
            acc = acc + v * v
        lines.append(jnp.sum(acc.T, axis=0, keepdims=True))
    squares[...] = jnp.concatenate(lines, axis=0)
    line = as_line(lines, sent[0].shape[1])
    for i in range(n):
        sent[i][LATENTS:, :] = line


def resample_sent(ids, features, latent_param, hidden, weights):
    n = ids.shape[0] - 2
    _, patches, vdim = features.shape
    _, rows, width = hidden.shape
    inner = weights[0].shape[1]
    return pl.pallas_call(
        functools.partial(resample_sent_kernel, n),
        out_shape=[pltpu.VMEM((LATENTS + SPARE, vdim), BF16)] * n
        + [pltpu.VMEM((2, rows), F32)],
        in_specs=[IN_SMEM, IN_VMEM, IN_VMEM] + [IN_HBM] * 5,
        out_specs=[IN_VMEM] * (n + 1),
        scratch_shapes=[pltpu.VMEM((rows, width), BF16)] * 2
        + [pltpu.SemaphoreType.DMA((2,))]
        + resample_scratch(n, patches, vdim, inner, weights),
        compiler_params=pltpu.CompilerParams(vmem_limit_bytes=24 * MIB),
        name="resample",
    )(ids, latent_param, near(features), away(hidden), *[away(w) for w in weights])


def resample_own_kernel(ids, lat, feat, *refs):
    refs[4][...] = resample_updates([feat.at[ids[0]]], lat, refs[:4], refs[5:9], *refs[9:])


def resample_own(ids, features, latent_param, weights):
    _, patches, vdim = features.shape
    inner = weights[0].shape[1]
    return pl.pallas_call(
        resample_own_kernel,
        out_shape=pltpu.VMEM((LATENTS, vdim), F32),
        in_specs=[IN_SMEM, IN_VMEM, IN_VMEM] + [IN_HBM] * 4,
        out_specs=IN_VMEM,
        scratch_shapes=resample_scratch(1, patches, vdim, inner, weights),
        compiler_params=pltpu.CompilerParams(vmem_limit_bytes=16 * MIB),
        name="resample",
    )(ids, latent_param, near(features), *[away(w) for w in weights])


def combine_kernel(lat, squares, own, a, b, c, out, total_squares):
    total = own[...]
    sums = squares[...]
    count = squares.shape[0]
    for part in (a, b, c):
        total = total + part[:LATENTS, :].astype(F32)
        line = part[LATENTS:, :].astype(F32)[0:1, :]
        at = lambda i: line[:, i * 128 : (i + 1) * 128]
        sums = sums + jnp.concatenate([at(i) + at(count + i) for i in range(count)], axis=0)
    out[...] = normalize(lat[...].astype(F32) + total).astype(BF16)
    total_squares[...] = sums


def combine(latent_param, squares, own, parts):
    return pl.pallas_call(
        combine_kernel,
        out_shape=[
            pltpu.VMEM(latent_param.shape, BF16),
            pltpu.VMEM(squares.shape, F32),
        ],
        in_specs=[IN_VMEM] * 6,
        out_specs=[IN_VMEM] * 2,
        compiler_params=pltpu.CompilerParams(vmem_limit_bytes=8 * MIB),
        name="combine",
    )(latent_param, squares, near(own), *[near(p) for p in parts])


TILE = 1024
AHEAD = 2


def project_kernel(count, moved, flags, *refs):
    chunks, refs = refs[:count], refs[count:]
    hid, own_k, own_v, other_k, other_v = refs[:5]
    keys, vals, tiles = refs[5:8]
    near_hid = refs[8 : 8 + moved]
    chosen, sems, hid_sems = refs[8 + moved :]
    steps = 2 * (keys.shape[1] // TILE)

    def fetch(step, src):
        cols = pl.ds(pl.multiple_of(step // 2 * TILE, TILE), TILE)
        return pltpu.make_async_copy(src.at[0, :, cols], tiles.at[step], sems.at[step])

    def start(step, odd):
        of_own, of_other = (own_v, other_v) if odd else (own_k, other_k)

        @pl.when(flags[0] == 0)
        def _():
            fetch(step, of_own).start()

        @pl.when(flags[0] != 0)
        def _():
            fetch(step, of_other).start()

    @pl.when(flags[1] != 0)
    def _():
        for step in range(AHEAD):
            start(step, step % 2)
        loads = [
            pltpu.make_async_copy(hid.at[flags[2 + i]], near_hid[i], hid_sems.at[i])
            for i in range(moved)
        ]
        for load in loads:
            load.start()
        top = 0
        for a in chunks:
            chosen[top : top + a.shape[0], :] = a[...]
            top += a.shape[0]

        def column(j, carry):
            cols = pl.ds(pl.multiple_of(j * TILE, TILE), TILE)
            for i, out in enumerate((keys, vals)):
                step = 2 * j + i
                fetch(step, own_k).wait()

                @pl.when(step + AHEAD < steps)
                def _():
                    start(step + AHEAD, (i + AHEAD) % 2)

                out[:, cols] = dot(chosen[...], tiles[step]).astype(BF16)
            return carry

        lax.fori_loop(0, steps // 2, column, 0)
        for load in loads:
            load.wait()


def project(flags, chunks, own, other, hidden, moved=0, keep=False):
    vdim, width = own[0].shape[1:]
    rows = sum(a.shape[0] for a in chunks)
    steps = 2 * (width // TILE)
    held = pltpu.VMEM((steps, vdim, TILE), BF16)
    kernel = functools.partial(project_kernel, len(chunks), moved)
    if not keep:
        inner = kernel

        def kernel(*refs):
            at = 1 + len(chunks) + 7
            refs, tiles = refs[:-1], refs[-1]
            return inner(*refs[:at], tiles, *refs[at:])

    return pl.pallas_call(
        kernel,
        out_shape=[pltpu.VMEM((rows, width), BF16)] * 2
        + [held] * keep
        + [pltpu.VMEM(hidden.shape[1:], BF16)] * moved,
        in_specs=[IN_SMEM] + [IN_VMEM] * len(chunks) + [IN_HBM] * 5,
        out_specs=[IN_VMEM] * (2 + keep + moved),
        scratch_shapes=[
            pltpu.VMEM((rows, vdim), BF16),
            pltpu.SemaphoreType.DMA((steps,)),
            pltpu.SemaphoreType.DMA((2,)),
        ]
        + [held] * (not keep),
        compiler_params=pltpu.CompilerParams(vmem_limit_bytes=(8 if keep else 20) * MIB),
        cost_estimate=pl.CostEstimate(
            flops=FEW, bytes_accessed=0, transcendentals=0
        ),
        name="project",
    )(flags, *[near(a) for a in chunks], *[away(a) for a in (hidden, *own, *other)])


def project_both_kernel(flags, a, b, own_k, own_v, other_k, other_v, k1, v1, k2, v2, chosen, ring, sems):
    part = a.shape[0]
    half = 2 * (k1.shape[1] // TILE)
    depth = ring.shape[0]

    def fetch(step, src):
        cols = pl.ds(pl.multiple_of(step % half // 2 * TILE, TILE), TILE)
        return pltpu.make_async_copy(src.at[0, :, cols], ring.at[step % depth], sems.at[step % depth])

    def start(step, odd):
        of_own, of_other = (own_v, other_v) if odd else (own_k, other_k)
        from_own = (step // half) == flags[0]

        @pl.when(from_own)
        def _():
            fetch(step, of_own).start()

        @pl.when(jnp.logical_not(from_own))
        def _():
            fetch(step, of_other).start()

    @pl.when(flags[1] != 0)
    def _():
        for step in range(depth - 1):
            start(step, step % 2)
        chosen[0:part, :] = a[...]
        chosen[part:, :] = b[...]
        for which, outs in enumerate(((k1, v1), (k2, v2))):

            def column(j, carry, which=which, outs=outs):
                cols = pl.ds(pl.multiple_of(j * TILE, TILE), TILE)
                for i, out in enumerate(outs):
                    step = which * half + 2 * j + i
                    fetch(step, own_k).wait()

                    @pl.when(step + depth - 1 < 2 * half)
                    def _():
                        start(step + depth - 1, (i + depth - 1) % 2)

                    out[:, cols] = dot(chosen[...], ring[step % depth]).astype(BF16)
                return carry

            lax.fori_loop(0, half // 2, column, 0)


def project_both(flags, a, b, own, other):
    vdim, width = own[0].shape[1:]
    rows = a.shape[0] + b.shape[0]
    return pl.pallas_call(
        project_both_kernel,
        out_shape=[pltpu.VMEM((rows, width), BF16)] * 4,
        in_specs=[IN_SMEM, IN_VMEM, IN_VMEM] + [IN_HBM] * 4,
        out_specs=[IN_VMEM] * 4,
        scratch_shapes=[
            pltpu.VMEM((rows, vdim), BF16),
            pltpu.VMEM((AHEAD + 1, vdim, TILE), BF16),
            pltpu.SemaphoreType.DMA((AHEAD + 1,)),
        ],
        compiler_params=pltpu.CompilerParams(vmem_limit_bytes=16 * MIB),
        cost_estimate=pl.CostEstimate(flops=FEW, bytes_accessed=0, transcendentals=0),
        name="project",
    )(flags, near(a), near(b), *[away(w) for w in (*own, *other)])


def project_held_kernel(flags, a, tiles, *refs):
    keys, vals = refs[-2:]

    @pl.when(flags[1] != 0)
    def _():
        def column(j, carry):
            cols = pl.ds(pl.multiple_of(j * TILE, TILE), TILE)
            keys[:, cols] = dot(a[...], tiles[2 * j]).astype(BF16)
            vals[:, cols] = dot(a[...], tiles[2 * j + 1]).astype(BF16)
            return carry

        lax.fori_loop(0, keys.shape[1] // TILE, column, 0)


def project_held(flags, a, tiles, after=()):
    steps, vdim, _ = tiles.shape
    rows = a.shape[0]
    width = steps // 2 * TILE
    return pl.pallas_call(
        project_held_kernel,
        out_shape=[pltpu.VMEM((rows, width), BF16)] * 2,
        in_specs=[IN_SMEM] + [IN_VMEM] * (2 + len(after)),
        out_specs=[IN_VMEM] * 2,
        compiler_params=pltpu.CompilerParams(vmem_limit_bytes=8 * MIB),
        cost_estimate=pl.CostEstimate(
            flops=FEW, bytes_accessed=0, transcendentals=0
        ),
        name="project",
    )(flags, near(a), near(tiles), *[near(b) for b in after])


def gather_kernel(*refs):
    for i, a in enumerate(refs[:-1]):
        refs[-1][i * LATENTS : (i + 1) * LATENTS, :] = a[...]


def gather(chunks):
    vdim = chunks[0].shape[1]
    return pl.pallas_call(
        gather_kernel,
        out_shape=pltpu.VMEM((len(chunks) * LATENTS, vdim), BF16),
        in_specs=[IN_VMEM] * len(chunks),
        out_specs=IN_VMEM,
        compiler_params=pltpu.CompilerParams(vmem_limit_bytes=2 * MIB),
        name="gather",
    )(*[near(a) for a in chunks])


def as_line(lines, width):
    high = [line.astype(BF16).astype(F32) for line in lines]
    low = [line - h for line, h in zip(lines, high)]
    parts = high + low
    spare = jnp.zeros((1, width - len(parts) * parts[0].shape[1]), F32)
    line = jnp.concatenate(parts + [spare], axis=1)
    first = lax.broadcasted_iota(jnp.int32, (SPARE, width), 0) == 0
    return jnp.where(first, line, 0.0).astype(BF16)


def from_line_kernel(x, *refs):
    out = refs[-1]
    line = x[x.shape[0] - SPARE :, :].astype(F32)[0:1, :]
    at = lambda i: line[:, i * 128 : (i + 1) * 128]
    count = out.shape[0]
    out[...] = jnp.concatenate([at(i) + at(count + i) for i in range(count)], axis=0)


def from_line(x, after):
    return pl.pallas_call(
        from_line_kernel,
        out_shape=pltpu.VMEM((1, 128), F32),
        in_specs=[IN_VMEM] * (1 + len(after)),
        out_specs=IN_VMEM,
        compiler_params=pltpu.CompilerParams(vmem_limit_bytes=2 * MIB),
        name="from_line",
    )(near(x), *[near(a) for a in after])


def layer_kernel(row, places, count, ahead, riding, others, routed, carried, *refs):
    batches = len(places)
    flags, refs = (refs[0], refs[1:]) if others else (None, refs)
    xs, metas, refs = refs[:batches], refs[batches : 2 * batches], refs[2 * batches :]
    keys, vals, refs = refs[0], refs[1], refs[2:]
    squares, before, refs = refs[:count], refs[count : count + ahead], refs[count + ahead :]
    alts, refs = refs[:others], refs[others + carried :]
    outs, refs = refs[: batches * (1 + routed)], refs[batches * (1 + routed) :]
    square_out, refs = refs[0], refs[1 + carried :]
    scale_s, bias_s, high_s, half_s, gate_s, acc = refs
    rows = metas[0].shape[1]
    heads = xs[0].shape[1] // HEAD
    slots = 4 * LATENTS

    def write(i, cols, old, new):
        if routed:
            outs[2 * i][:, cols] = jnp.where(flags[1] == 0, old, new)
            outs[2 * i + 1][:, cols] = jnp.where(flags[1] == 0, new, old)
        else:
            outs[i][0:rows, cols] = new

    def run():
        total = squares[0][...]
        for part in squares[1:]:
            total = total + part[...]
        ones = jnp.ones((slots, HEAD), BF16)
        lines = [b[...] for b in before]
        for i, (at, line) in enumerate(places):
            scale = lax.rsqrt(total[line : line + 1, :] / D + EPS) * (HEAD ** (-0.5) * LOG2E)
            spare = jnp.zeros((rows - 3, rows), F32)
            gate = metas[i][row : row + 1, :]
            cols = jnp.concatenate([scale, metas[i][0:1, :], gate, spare], axis=0).T
            slot = jnp.broadcast_to(cols[:, 1:2], (rows, HEAD))
            scale_s[...] = jnp.broadcast_to(cols[:, 0:1], (rows, HEAD))
            gate_s[...] = jnp.broadcast_to(cols[:, 2:3], (rows, HEAD))
            upper = jnp.where(slot > 1.5, 1.0, 0.0)
            high_s[...] = upper
            half_s[...] = upper.astype(BF16)
            half = (lax.broadcasted_iota(jnp.int32, (rows, HEAD), 1) // LATENTS).astype(F32)
            bias_s[...] = jnp.where(slot - 2.0 * upper == half, 0.0, NEG)
            high = high_s[...] > 0.5
            sums = jnp.zeros((rows, HEAD), F32)
            for h in range(heads):
                cols = slice(h * HEAD, (h + 1) * HEAD)
                k = keys[at * slots : (at + 1) * slots, cols]
                v = vals[at * slots : (at + 1) * slots, cols]
                q = xs[i][0:rows, cols]
                score = dot_nt(q, k)
                t = jnp.where(high, score[:, HEAD:], score[:, :HEAD]) * scale_s[...] + bias_s[...]
                e = jnp.exp2(t - jnp.max(t, axis=1, keepdims=True)).astype(BF16)
                e_high = e * half_s[...]
                weight = jnp.concatenate([e - e_high, e_high], axis=1)
                mixed = dot(weight, jnp.concatenate([v, ones], axis=1))
                attn = mixed[:, :HEAD] / mixed[:, HEAD:]
                out = (q.astype(F32) + gate_s[...] * attn).astype(BF16)
                write(i, cols, q, out)
                of = out.astype(F32)
                sums = sums + of * of
            acc[...] = sums
            lines.append(jnp.sum(acc[...].T, axis=0, keepdims=True))
        square_out[...] = jnp.concatenate(lines, axis=0)
        if riding:
            outs[-1][rows:, :] = as_line(lines, outs[-1].shape[1])

    if not others:
        run()
        return
    pl.when(flags[0] != 0)(run)

    @pl.when(flags[0] == 0)
    def _():
        for i in range(batches):
            for h in range(heads):
                cols = slice(h * HEAD, (h + 1) * HEAD)
                write(i, cols, alts[i][0:rows, cols], alts[batches + i][0:rows, cols])
        square_out[...] = jnp.zeros_like(square_out)


def layer(
    row, xs, metas, kv, places, squares, before=(), riding=False, flags=None, alts=(), routed=False, carry=()
):
    keys, vals = kv
    rows = metas[0].shape[1]
    width = xs[0].shape[1]
    slots = 4 * LATENTS
    batches = len(xs)
    scratch = pltpu.VMEM((rows, HEAD), F32)
    ys = [pltpu.VMEM((rows, width), BF16)] * (batches * (1 + routed))
    if riding:
        ys[-1] = pltpu.VMEM((rows + SPARE, width), BF16)
    switch = [] if flags is None else [flags]
    first = len(switch) + 2 + 2 * batches + len(squares) + len(before) + len(alts)
    return pl.pallas_call(
        functools.partial(
            layer_kernel,
            row,
            places,
            len(squares),
            len(before),
            riding,
            len(alts),
            routed,
            len(carry),
        ),
        out_shape=ys
        + [pltpu.VMEM((batches + len(before), rows), F32)]
        + [pltpu.VMEM(a.shape, a.dtype) for a in carry],
        in_specs=[IN_SMEM] * len(switch) + [IN_VMEM] * (first - len(switch) + len(carry)),
        out_specs=[IN_VMEM] * (len(ys) + 1 + len(carry)),
        scratch_shapes=[scratch] * 3 + [pltpu.VMEM((rows, HEAD), BF16)] + [scratch] * 2,
        input_output_aliases={first + i: len(ys) + 1 + i for i in range(len(carry))},
        compiler_params=pltpu.CompilerParams(vmem_limit_bytes=8 * MIB),
        cost_estimate=pl.CostEstimate(
            flops=FEW, bytes_accessed=0, transcendentals=0,
        ),
        name="layer",
    )(
        *switch,
        *[near(x) for x in xs],
        *metas,
        near(keys),
        near(vals),
        *[near(a) for a in (*squares, *before, *alts, *carry)],
    )


def place_kernel(lead, core, *refs):
    a, b, out, sems = refs[lead:]
    copies = [
        pltpu.make_async_copy(a, out.at[core[0]], sems.at[0]),
        pltpu.make_async_copy(b, out.at[core[0] ^ 1], sems.at[1]),
    ]
    for copy in copies:
        copy.start()
    for copy in copies:
        copy.wait()


def place(at, a, b, onto=None):
    lead = 0 if onto is None else 1
    return pl.pallas_call(
        functools.partial(place_kernel, lead),
        out_shape=jax.ShapeDtypeStruct((4, *a.shape), a.dtype),
        in_specs=[IN_SMEM] + [IN_HBM] * lead + [IN_VMEM] * 2,
        out_specs=IN_HBM,
        scratch_shapes=[pltpu.SemaphoreType.DMA((2,))],
        input_output_aliases={1: 0} if lead else {},
        compiler_params=pltpu.CompilerParams(vmem_limit_bytes=2 * MIB),
        name="place",
    )(at[None].astype(jnp.int32), *([] if onto is None else [onto]), near(a), near(b))


def body(
    features,
    latent_param,
    query_proj,
    key_proj,
    value_proj,
    out_proj,
    hidden,
    key_weight,
    value_weight,
    gate_angle,
    group_images,
    token_slot,
    attend,
):
    s = lax.axis_index("section")
    c = lax.axis_index("seq")
    m = lax.axis_index("mp")
    core = s & 1
    far = s >> 1
    mates = lax.axis_size("mp")
    seqs = lax.axis_size("seq")
    sections = lax.axis_size("section")

    def mp_swap(a, k):
        return lax.ppermute(a, "mp", [(i, i ^ k) for i in range(mates)])

    def core_swap(a):
        return lax.ppermute(a, "section", [(i, i ^ 1) for i in range(sections)])

    def far_swap(a):
        return lax.ppermute(a, "section", [(i, i ^ 2) for i in range(sections)])

    def cross(a):
        return lax.ppermute(a, "section", [(0, 2), (1, 3)])

    def spread(a):
        return [a] + [mp_swap(a, k) for k in (1, 2, 3)]

    other_w = (core_swap(key_weight), core_swap(value_weight))
    gate_own = jnp.broadcast_to(jnp.tanh(gate_angle)[:, None], (1, 128))
    gate_other = core_swap(gate_own)
    gate_first = jnp.where(core == 0, gate_own, gate_other)
    gate_second = jnp.where(core == 0, gate_other, gate_own)

    order = jnp.stack([m ^ 2, m ^ 1, m ^ 3, core, core + 2]).astype(jnp.int32)
    weights = (query_proj, key_proj, value_proj, out_proj)
    p2, p1, p3, squares = resample_sent(order, features, latent_param, hidden, weights)
    r2, r1, r3 = mp_swap(p2, 2), mp_swap(p1, 1), mp_swap(p3, 3)
    p0 = resample_own(m[None].astype(jnp.int32), features, latent_param, weights)
    latents, entering = combine(latent_param, squares, p0, (r1, r2, r3))

    inner = [(i, i ^ 1) for i in range(seqs)]
    outer = [(i, (((i + 1) ^ 1) - 1) % seqs) for i in range(seqs)]
    in_pair = lax.ppermute(latents, "seq", inner)
    across = lax.ppermute(latents, "seq", outer)
    odd = (c & 1) == 1
    firsts = group_images[:, 0, 0]
    start = lax.dynamic_index_in_dim(firsts, s, 0, keepdims=False)
    where_is = ((start + ((m - start) & 3)) >> 2) - c
    picked = jnp.where(
        where_is == 0, latents, jnp.where((where_is < 0) == odd, in_pair, across)
    )
    own_set = gather(spread(picked))
    far_set = far_swap(own_set)

    block = m ^ ((firsts[:, None] + token_slot[:, 0, :]) & 3)
    alive = attend[:, 0, :].astype(F32)
    rows = jnp.stack(
        [block.astype(F32), alive * gate_first, alive * gate_second]
        + [jnp.zeros_like(alive)] * 5,
        axis=1,
    )
    meta_own = lax.dynamic_index_in_dim(rows, s, 0, keepdims=False)
    meta_far = lax.dynamic_index_in_dim(rows, s ^ 2, 0, keepdims=False)

    own_w = (key_weight, value_weight)
    is_near = 1 - far

    flags = jnp.stack([core, is_near, core, core + 2]).astype(jnp.int32)
    flags_second = jnp.stack([1 - core, is_near]).astype(jnp.int32)
    k, v, tiles, hidden0, hidden1 = project(
        flags, [own_set], own_w, other_w, hidden, moved=2, keep=True
    )
    a0, qa0 = layer(1, [hidden0], [meta_own], (k, v), ((0, 0),), [entering])
    *second, tiles_second = project(flags_second, [own_set], own_w, other_w, hidden, keep=True)
    b0, _ = layer(2, [a0], [meta_own], second, ((0, 0),), spread(qa0), riding=True)
    x0 = cross(b0)
    kv = project_held(flags, far_set, tiles, [b0])
    a1, qa1 = layer(1, [hidden1], [meta_far], kv, ((0, 1),), [entering])
    kv = project_held(flags_second, far_set, tiles_second)
    b1, _ = layer(2, [a1], [meta_far], kv, ((0, 0),), spread(qa1), riding=True)
    x1 = cross(b1)

    flags = jnp.stack([core, far]).astype(jnp.int32)
    kv = project_both(flags, own_set, far_set, own_w, other_w)
    first, second = kv[:2], kv[2:]
    flags = jnp.stack([far, core]).astype(jnp.int32)
    c0, qc0, *second = layer(
        1, [x0], [meta_far], first, ((1, 0),), spread(from_line(x0, (b1, *first, *second))), carry=second
    )
    keep0, send0, _, *second = layer(
        2,
        [c0],
        [meta_far],
        second,
        ((1, 0),),
        spread(qc0),
        flags=flags,
        alts=(a0, b0),
        routed=True,
        carry=second,
    )
    c1, qc1 = layer(1, [x1], [meta_own], first, ((0, 0),), spread(from_line(x1, ())))
    keep1, send1, _ = layer(
        2, [c1], [meta_own], second, ((0, 0),), spread(qc1), flags=flags, alts=(a1, b1), routed=True
    )

    got0, got1 = core_swap(send0), core_swap(send1)
    out = place(core, keep0, got0)
    return place(core + 2, keep1, got1, out)[None]


def solution(mesh):
    return jax.shard_map(
        body,
        mesh=mesh,
        in_specs=(
            P(("section", "seq"), None, None),
            P(),
            P(None, "mp"),
            P(None, "mp"),
            P(None, "mp"),
            P("mp", None),
            P(None, "seq", "mp"),
            P("section", None, "mp"),
            P("section", None, "mp"),
            P("section"),
            P(None, "seq", None),
            P(None, "seq", None),
            P(None, "seq", None),
        ),
        out_specs=P("section", None, "seq", "mp"),
        check_vma=False,
    )
```
